32 devices in a mesh: layer: 2 (over y), feat: 4 (over z), width: 4 (over x, core).
Axes of the slice: x: 2, y: 2, z: 4, core: 2. Of those that a mesh axis runs over, the one named last changes fastest.
Arguments:
- inputs: float32 [2, 1024, 2048], P('layer', None, 'width'), may hold values from -6 to 6
- targets: float32 [2, 1024, 2048], P(None, ('layer', 'feat'), 'width'), may hold values from -6 to 6
- w_enc: float32 [2, 2048, 16384], P('layer', 'width', 'feat'), may hold values from -0.125 to 0.125
- b_enc: float32 [2, 16384], P('layer', 'feat'), may hold values from -3 to 3
- thresholds: float32 [2, 16384], P('layer', 'feat'), may hold values from 0.2 to 1
- w_dec: float32 [2, 2, 16384, 2048], P('layer', None, 'feat', 'width'), may hold values from -0.046875 to 0.046875
- b_dec: float32 [2, 2048], P(None, 'width'), may hold values from -3 to 3
Outputs:
- dec_grad: float32 [2, 2, 16384, 2048], P('layer', None, 'feat', 'width')
- pre_grad: float32 [2, 1024, 16384], P('layer', 'width', 'feat')
The draws below stay inside these ranges and needn't reach their ends.
All inputs are finite; a program needn't handle non-finite values.
Results may differ from the reference program's by a relative error of at most 0.0001.
Values sent between devices are 32-bit elements; how exact they have to be, the bound alone decides.
No kernel may reach another device: no remote copies, remote signals or barrier semaphores. Data moves between devices by JAX's collectives and lax.ppermute only.
A program may use at most 192 MiB of HBM per device.

```python
import jax
import jax.numpy as jnp
from jax import lax

D = 2048
F = 16384
TOK = 1024
LAYERS = 2


def level_of(stream_key, shape, shards, smallest, largest):
    gain = 1.0
    for dim, blocks in shards:
        draws = jax.random.uniform(jax.random.fold_in(jax.random.fold_in(stream_key, 6), dim), (blocks,), jnp.float32, smallest / len(shards), largest / len(shards))
        gain = gain * jnp.repeat(jnp.exp(draws), shape[dim] // blocks).reshape((-1,) + (1,) * (len(shape) - 1 - dim))
    return gain


def noise(own_key, extent, width, limit, cuts=(), kind=jnp.bfloat16):
    level = level_of(own_key, extent, cuts, -0.22, 0.18) if cuts else 1.0
    array = jax.random.normal(own_key, extent, jnp.float32) * width * level
    return jnp.minimum(jnp.maximum(array, -limit), limit).astype(kind)


def setup_inputs(seed: int = 0) -> dict:
    streams_of = jax.random.split(jax.random.key(seed), 8)
    return {
        "inputs": noise(streams_of[0], (LAYERS, TOK, D), 1.0, 6.0, ((0, 2), (2, 4)), jnp.float32),
        "targets": noise(streams_of[1], (LAYERS, TOK, D), 1.0, 6.0, ((1, 8), (2, 4)), jnp.float32),
        "w_enc": noise(streams_of[2], (LAYERS, D, F), D ** -0.5, 0.125, ((0, 2), (1, 4), (2, 4)), jnp.float32),
        "b_enc": noise(streams_of[3], (LAYERS, F), 0.5, 3.0, ((0, 2), (1, 4)), jnp.float32),
        "thresholds": jnp.clip(0.2 + 0.8 * jax.random.uniform(streams_of[4], (LAYERS, F), jnp.float32) ** level_of(streams_of[4], (LAYERS, F), ((0, 2), (1, 4)), -0.2, 0.2), 0.2, 1.0),
        "w_dec": noise(streams_of[5], (LAYERS, LAYERS, F, D), F ** -0.5, 0.046875, ((0, 2), (2, 4), (3, 4)), jnp.float32),
        "b_dec": noise(streams_of[6], (LAYERS, D), 0.5, 3.0, ((1, 4),), jnp.float32),
    }


softness = 0.5


def reference(inputs, targets, w_enc, b_enc, thresholds, w_dec, b_dec):
    highest = lax.Precision.HIGHEST
    pre_act = jnp.einsum('lnd,ldf->lnf', inputs, w_enc, precision=highest) + b_enc[:, None, :]
    gate_open = jax.nn.sigmoid((pre_act - thresholds[:, None, :]) / softness)
    activations = pre_act * gate_open
    slope_val = gate_open + pre_act * gate_open * (1.0 - gate_open) / softness
    errors = []
    for target_pos in range(LAYERS):
        recon = b_dec[target_pos][None, :] - targets[target_pos]
        for source_pos in range(target_pos + 1):
            recon = recon + jnp.dot(activations[source_pos], w_dec[source_pos, target_pos], precision=highest, preferred_element_type=jnp.float32)
        errors.append(recon)
    grad_rows = []
    back_rows = []
    for source_pos in range(LAYERS):
        per_target = []
        back_sum = jnp.zeros(activations.shape[1:], activations.dtype)
        for target_pos in range(LAYERS):
            if target_pos >= source_pos:
                per_target.append(lax.dot_general(activations[source_pos], errors[target_pos], (((0,), (0,)), ((), ())), precision=highest, preferred_element_type=jnp.float32))
                back_sum = back_sum + lax.dot_general(errors[target_pos], w_dec[source_pos, target_pos], (((1,), (1,)), ((), ())), precision=highest, preferred_element_type=jnp.float32)
            else:
                per_target.append(jnp.zeros(w_dec.shape[2:], w_dec.dtype))
        grad_rows.append(jnp.stack(per_target))
        back_rows.append(back_sum * slope_val[source_pos])
    return jnp.stack(grad_rows), jnp.stack(back_rows)
```

```python
import functools

import jax
import jax.numpy as jnp
from jax import lax
from jax.experimental import pallas as pl
from jax.experimental.pallas import tpu as pltpu
from jax.sharding import PartitionSpec as P

softness = 0.5
eighths = (1, 1, 2, 2, 1, 1)
cuts = 4
f32 = jnp.float32
bf16 = jnp.bfloat16
anywhere = pl.BlockSpec(memory_space=pl.ANY)
scalars = pl.BlockSpec(memory_space=pltpu.SMEM)
vector = pl.BlockSpec(memory_space=pltpu.VMEM)
hbm = pl.BlockSpec(memory_space=pltpu.HBM)
granted = 46 * 1024 * 1024


def pieces_of(rows):
    if rows % 128:
        return [(0, rows)]
    bounds = [0]
    for part in eighths:
        bounds.append(bounds[-1] + part * rows // 8)
    return list(zip(bounds[:-1], bounds[1:]))


def halves(value):
    high = value.astype(bf16)
    return high, (value - high.astype(f32)).astype(bf16)


def three(a_high, a_low, b_high, b_low, dims):
    dot = functools.partial(
        lax.dot_general, dimension_numbers=(dims, ((), ())), preferred_element_type=f32
    )
    return dot(a_high, b_high) + (dot(a_low, b_high) + dot(a_high, b_low))


plain = ((1,), (0,))
across_rows = ((0,), (0,))
across_columns = ((1,), (1,))


def shape(dims, kind=f32):
    return jax.ShapeDtypeStruct(dims, kind)


def loop(total, step, body):
    def turn(k, carry):
        body(pl.ds(pl.multiple_of(k * step, step), step))
        return carry

    lax.fori_loop(0, total // step, turn, 0)


def join(refs, columns):
    return jnp.concatenate([r[:, columns] for r in refs])


class Chain:
    def __init__(self):
        self.last = None

    def __call__(
        self, name, body, inputs, outputs, scratch=(), aliases=None, grid=None
    ):
        arrays = [a for a, _ in inputs]
        in_specs = [s for _, s in inputs]
        extra = 0
        if self.last is not None:
            arrays.append(self.last)
            in_specs.append(anywhere)
            extra = 1
        count = len(inputs)
        given = len(outputs)

        def kernel(*refs):
            ins = refs[:count]
            outs = refs[count + extra : count + extra + given]
            mark = refs[count + extra + given]
            mark[...] = jnp.zeros_like(mark)
            body(ins, outs, *refs[count + extra + given + 1 :])

        mark_spec = vector if grid is None else pl.BlockSpec((8, 128), lambda *i: (0, 0))
        result = pl.pallas_call(
            kernel,
            grid=grid or (),
            in_specs=in_specs,
            out_specs=[s for _, s in outputs] + [mark_spec],
            out_shape=[o for o, _ in outputs] + [shape((8, 128))],
            scratch_shapes=list(scratch),
            input_output_aliases=aliases or {},
            compiler_params=pltpu.CompilerParams(vmem_limit_bytes=granted),
            cost_estimate=pl.CostEstimate(flops=0, bytes_accessed=0, transcendentals=0),
            name=name,
        )(*arrays)
        self.last = result[-1]
        return result[:-1]


def stream(count, copy, body):
    copy(0).start()
    for k in range(count):
        if k + 1 < count:
            copy(k + 1).start()
        copy(k).wait()
        body(k, k % 2)


def local(inputs, targets, w_enc, b_enc, thresholds, w_dec, b_dec):
    layer_pos = lax.axis_index("layer")
    first = layer_pos == 0
    feat_pos = lax.axis_index("feat")
    feat_size = lax.axis_size("feat")
    width = lax.axis_size("width")
    pos = lax.axis_index("width")
    near = pos % 2
    far = pos // 2
    tokens = inputs.shape[1]
    model = inputs.shape[2]
    feats = w_enc.shape[2]
    share = tokens // width
    tile = min(512, feats)
    wide = min(1024, feats)
    wides = feats // wide
    group = min(model, wide)
    groups = wide // group
    shared = (groups * model, group) == (wide, model)
    blocks = 3 * wides if shared else wides
    skipped = wides if shared else 0
    near_pairs = [(i, i ^ 1) for i in range(width)]
    far_pairs = [(i, i ^ 2) for i in range(width)]
    pieces = pieces_of(share)
    flags = jnp.stack([first.astype(jnp.int32), far.astype(jnp.int32)])

    def swap_near(arrays):
        return [lax.ppermute(a, "width", near_pairs) for a in arrays]

    def swap_far(a):
        return lax.ppermute(a, "width", far_pairs)

    def arrange(rows):
        split = rows.reshape(2, 2, share, rows.shape[-1])
        found = []
        for lo, hi in pieces:
            cut = split[:, :, lo:hi]
            own = lax.dynamic_index_in_dim(cut, near, 1, keepdims=False)
            other = lax.dynamic_index_in_dim(cut, 1 - near, 1, keepdims=False)
            found.append(jnp.stack([own, other]).reshape(-1, model))
        return found

    x_rows = arrange(inputs[0])
    chain = Chain()
    store = [{} for _ in pieces]
    weights = {}
    saved = {}

    def size(i):
        return pieces[i][1] - pieces[i][0]

    def cut_rows(i):
        return 2 * size(i) // cuts

    def cut_shapes(i):
        return [(shape((cut_rows(i), feats)), vector)] * cuts

    def write_cuts(i, value, own, others, columns):
        n = size(i)
        own[:, columns] = value[: 2 * n]
        for k, out in enumerate(others):
            start = 2 * n + k * cut_rows(i)
            out[:, columns] = value[start : start + cut_rows(i)]

    def fetch(source, buffers, sems):
        return lambda k: pltpu.make_async_copy(source.at[k], buffers.at[k % 2], sems.at[k % 2])

    def fetch_pairs(source, buffers, sems):
        return lambda k: pltpu.make_async_copy(
            source.at[pl.ds(skipped + 2 * k, 2)], buffers.at[k % 2], sems.at[k % 2]
        )

    def enter(i):
        n = size(i)

        def body(ins, outs, buffers, made, sems):
            x, w = ins
            own, *others, kept = outs
            x_high, x_low = halves(x[...])

            def read(k):
                return pltpu.make_async_copy(
                    w.at[0, :, pl.ds(k * wide, wide)], buffers.at[k % 2], sems.at[k % 2]
                )

            def write(k):
                return pltpu.make_async_copy(made.at[k % 2], kept.at[k], sems.at[2 + k % 2])

            def step(k, slot):
                w_high, w_low = halves(buffers[slot])
                if k >= 2:
                    write(k - 2).wait()
                for g in range(groups):
                    rows, cut = slice(g * model, (g + 1) * model), slice(g * group, (g + 1) * group)
                    made[slot, 0, rows], made[slot, 1, rows] = w_high[:, cut], w_low[:, cut]
                write(k).start()
                columns = slice(k * wide, (k + 1) * wide)
                write_cuts(i, three(x_high, x_low, w_high, w_low, plain), own, others, columns)

            stream(wides, read, step)
            for k in range(max(wides - 2, 0), wides):
                write(k).wait()

        own, *others, weights["enc"] = chain(
            "enter",
            body,
            [(x_rows[i], vector), (w_enc, hbm)],
            [(shape((2 * n, feats)), vector)]
            + cut_shapes(i)
            + [(shape((blocks, 2, groups * model, group), bf16), hbm)],
            scratch=[
                pltpu.VMEM((2, model, wide), f32),
                pltpu.VMEM((2, 2, groups * model, group), bf16),
                pltpu.SemaphoreType.DMA((4,)),
            ],
        )
        store[i]["own"], store[i]["in"] = own, swap_near(others)

    def part(i):
        n = size(i)

        def body(ins, outs, buffers, sems):
            x, w = ins
            own, *others = outs

            def step(k, slot):
                x_high, x_low = halves(x[...])
                for g in range(groups):
                    rows = slice(g * model, (g + 1) * model)
                    value = three(x_high, x_low, buffers[slot, 0, rows], buffers[slot, 1, rows], plain)
                    start = k * wide + g * group
                    write_cuts(i, value, own, others, slice(start, start + group))

            stream(wides, fetch(w, buffers, sems), step)

        own, *others = chain(
            "part",
            body,
            [(x_rows[i], vector), (weights["enc"], hbm)],
            [(shape((2 * n, feats)), vector)] + cut_shapes(i),
            scratch=[
                pltpu.VMEM((2, 2, groups * model, group), bf16),
                pltpu.SemaphoreType.DMA((2,)),
            ],
        )
        store[i]["own"], store[i]["in"] = own, swap_near(others)

    def summed(i):
        n = size(i)

        def body(ins, outs):
            own, *others = ins

            def step(columns):
                outs[0][:, columns] = own[:, columns] + join(others, columns)

            loop(feats, wide, step)

        (value,) = chain(
            "chip_sum",
            body,
            [(a, vector) for a in [store[i]["own"], *store[i]["in"]]],
            [(shape((2 * n, feats)), vector)],
        )
        store[i]["sum"], store[i]["in"] = value, swap_far(value)

    def split_decoder():
        def body(ins, outs, buffers, made, sems):
            w, kept = ins[0], outs[0]

            def read(k):
                return pltpu.make_async_copy(
                    w.at[0, :, pl.ds(k * wide, wide)], buffers.at[k % 2], sems.at[k % 2]
                )

            def write(k):
                return pltpu.make_async_copy(
                    made.at[k % 2], kept.at[pl.ds(skipped + 2 * k, 2)], sems.at[2 + k % 2]
                )

            def step(k, slot):
                if k >= 2:
                    write(k - 2).wait()
                for t in range(2):
                    made[slot, t, 0], made[slot, t, 1] = halves(buffers[slot, t])
                write(k).start()

            stream(wides, read, step)
            for k in range(max(wides - 2, 0), wides):
                write(k).wait()

        (weights["dec"],) = chain(
            "split_decoder",
            body,
            [(w_dec, hbm)] + ([(weights["enc"], hbm)] if shared else []),
            [(shape((skipped + 2 * wides, 2, wide, model), bf16), hbm)],
            aliases={1: 0} if shared else {},
            scratch=[
                pltpu.VMEM((2, 2, wide, model), f32),
                pltpu.VMEM((2, 2, 2, wide, model), bf16),
                pltpu.SemaphoreType.DMA((4,)),
            ],
        )
        if shared:
            weights["enc"] = weights["dec"]

    def goals():
        share_rows = targets.shape[1]

        def body(ins, outs):
            flag, goal = ins
            home, away = outs
            own = flag[0] == 1
            home[...] = jnp.where(own, goal[0], goal[1])
            away[...] = jnp.where(own, goal[1], goal[0])

        home, away = chain(
            "targets",
            body,
            [(flags, scalars), (targets, vector)],
            [(shape((share_rows, model)), vector)] * 2,
        )
        away = lax.ppermute(away, "layer", [(0, 1), (1, 0)])
        padded = jnp.zeros((tokens, model), f32)
        home_start = (layer_pos * feat_size + feat_pos) * share_rows
        away_start = ((1 - layer_pos) * feat_size + feat_pos) * share_rows
        padded = lax.dynamic_update_slice(padded, home, (home_start, jnp.int32(0)))
        padded = lax.dynamic_update_slice(padded, away, (away_start, jnp.int32(0)))
        weights["goal"] = arrange(padded)

    def gate(i):
        n = size(i)

        def body(ins, outs):
            flag, s, r, b, th = ins
            *acts, slope = outs

            def step(columns):
                bias, edge = b[:, columns], th[:, columns]

                def opened(pre):
                    return jax.nn.sigmoid((pre - edge) / softness)

                for k, out in enumerate(acts):
                    rows = slice(k * cut_rows(i), (k + 1) * cut_rows(i))
                    pre = s[rows, columns] + r[rows, columns] + bias
                    out[:, columns] = pre * opened(pre)
                rows = pl.ds(pl.multiple_of(flag[1] * n, n), n)
                pre = s[rows, columns] + r[rows, columns] + bias
                own = opened(pre)
                slope[:, columns] = own + pre * own * (1.0 - own) / softness

            loop(feats, wide, step)

        *acts, slope = chain(
            "gate",
            body,
            [
                (flags, scalars),
                (store[i]["sum"], vector),
                (store[i]["in"], vector),
                (b_enc, vector),
                (thresholds, vector),
            ],
            cut_shapes(i) + [(shape((n, feats)), vector)],
        )
        store[i]["acts"], store[i]["slope"], store[i]["in"] = acts, slope, swap_near(acts)

    def keep(name, ins, outs, columns):
        aliases = {}
        if name in saved:
            aliases = {len(ins): len(outs)}
            ins.append((saved[name], hbm))
        outs.append((shape((2, tokens, columns), bf16), hbm))
        return aliases

    def recon(i):
        n = size(i)
        lo = pieces[i][0]

        def body(ins, outs, buffers, made, sems):
            own, other, w = ins[:cuts], ins[cuts : 2 * cuts], ins[2 * cuts]
            r0, r1, kept = outs

            def save(k):
                rows, columns = pl.ds(4 * lo, 4 * n), pl.ds(k * wide, wide)
                return pltpu.make_async_copy(
                    made.at[k % 2], kept.at[:, rows, columns], sems.at[2 + k % 2]
                )

            def step(k, slot):
                columns = slice(k * wide, (k + 1) * wide)
                a_high, a_low = halves(join(own + other, columns))
                if k >= 2:
                    save(k - 2).wait()
                made[slot, 0], made[slot, 1] = a_high, a_low
                save(k).start()
                for t, out in enumerate((r0, r1)):
                    value = three(a_high, a_low, buffers[slot, t, 0], buffers[slot, t, 1], plain)
                    out[...] = out[...] + value if k else value

            stream(wides, fetch_pairs(w, buffers, sems), step)
            for k in range(max(wides - 2, 0), wides):
                save(k).wait()

        ins = [(a, vector) for a in [*store[i]["acts"], *store[i]["in"]]] + [(weights["dec"], hbm)]
        outs = [(shape((4 * n, model)), vector)] * 2
        aliases = keep("acts", ins, outs, feats)
        r0, r1, saved["acts"] = chain(
            "recon",
            body,
            ins,
            outs,
            scratch=[pltpu.VMEM((2, 2, 2, wide, model), bf16)]
            + [pltpu.VMEM((2, 2, 4 * n, wide), bf16)]
            + [pltpu.SemaphoreType.DMA((4,))],
            aliases=aliases,
        )
        store[i]["r"] = (r0, r1)
        store[i]["in"] = lax.ppermute(r1, "layer", [(0, 1)])

    def held(i):
        n = size(i)

        def body(ins, outs):
            flag, r0, r1, below, goal = ins
            outs[0][...] = jnp.where(flag[0] == 1, r0[...], r1[...] + below[...]) - goal[...]

        arrays = [*store[i]["r"], store[i]["in"], weights["goal"][i]]
        (value,) = chain(
            "held",
            body,
            [(flags, scalars)] + [(a, vector) for a in arrays],
            [(shape((4 * n, model)), vector)],
        )
        store[i]["held"] = value
        if feat_size <= 4:
            store[i]["in"] = lax.ppermute(value, "feat", [(k, k ^ 1) for k in range(feat_size)])
        else:
            store[i]["in"] = lax.psum(value, "feat")
            store[i]["held"] = jnp.zeros_like(value)

    def middle(i):
        n = size(i)
        if feat_size > 4:
            return

        def body(ins, outs):
            outs[0][...] = ins[0][...] + ins[1][...]

        (value,) = chain(
            "feat_sum",
            body,
            [(store[i]["held"], vector), (store[i]["in"], vector)],
            [(shape((4 * n, model)), vector)],
        )
        store[i]["held"] = value
        store[i]["in"] = lax.ppermute(value, "feat", [(k, k ^ 2) for k in range(feat_size)])

    def across(i):
        n = size(i)

        def body(ins, outs):
            flag, a, b, bias = ins
            line = jnp.where(flag[0] == 1, bias[0:1, :], bias[1:2, :])
            outs[0][...] = a[...] + b[...] + line

        (value,) = chain(
            "errors",
            body,
            [(flags, scalars)] + [(a, vector) for a in (store[i]["held"], store[i]["in"], b_dec)],
            [(shape((4 * n, model)), vector)],
        )
        store[i]["held"] = value
        store[i]["in"] = lax.ppermute(value, "layer", [(1, 0)])

    def back(i):
        n = size(i)
        lo = pieces[i][0]

        def body(ins, outs, buffers, made, sems):
            flag, value, above, w = ins[:4]
            own, *others, kept = outs
            e_high, e_low = made.at[0], made.at[1]
            is_first = flag[0] == 1
            zero = jnp.where(is_first, value[...], 0.0)
            one = jnp.where(is_first, above[...], value[...])
            e_high[:, :model], e_low[:, :model] = halves(zero)
            e_high[:, model:], e_low[:, model:] = halves(one)
            copy = pltpu.make_async_copy(made, kept.at[:, pl.ds(4 * lo, 4 * n)], sems.at[2])
            copy.start()

            def step(k, slot):
                total = None
                for t in range(2):
                    cut = slice(t * model, (t + 1) * model)
                    high, low = buffers[slot, t, 0], buffers[slot, t, 1]
                    term = three(e_high[:, cut], e_low[:, cut], high, low, across_columns)
                    total = term if total is None else total + term
                write_cuts(i, total, own, others, slice(k * wide, (k + 1) * wide))

            stream(wides, fetch_pairs(w, buffers, sems), step)
            copy.wait()

        arrays = [store[i]["held"], store[i]["in"]]
        ins = [(flags, scalars)] + [(a, vector) for a in arrays] + [(weights["dec"], hbm)]
        outs = [(shape((2 * n, feats)), vector)] + cut_shapes(i)
        aliases = keep("errors", ins, outs, 2 * model)
        own, *others, saved["errors"] = chain(
            "back",
            body,
            ins,
            outs,
            scratch=[pltpu.VMEM((2, 2, 2, wide, model), bf16)]
            + [pltpu.VMEM((2, 4 * n, 2 * model), bf16)]
            + [pltpu.SemaphoreType.DMA((3,))],
            aliases=aliases,
        )
        store[i]["own"], store[i]["in"] = own, swap_near(others)

    def turn(i):
        n = size(i)
        half = cuts // 2

        def body(ins, outs):
            flag, own, *others = ins
            mine, theirs = outs
            for place in range(2):

                @pl.when(flag[1] == place)
                def _():
                    for out, at in ((mine, place), (theirs, 1 - place)):

                        def step(columns):
                            arrived = join(others[at * half : (at + 1) * half], columns)
                            out[:, columns] = own[at * n : (at + 1) * n, columns] + arrived

                        loop(feats, wide, step)

        mine, theirs = chain(
            "turn",
            body,
            [(flags, scalars)] + [(a, vector) for a in [store[i]["own"], *store[i]["in"]]],
            [(shape((n, feats)), vector)] * 2,
        )
        store[i]["own"], store[i]["in"] = mine, swap_far(theirs)

    def finish(i):
        lo, hi = pieces[i]
        n = size(i)

        def body(ins, outs, value, sem):
            mine, arrived, slope = ins[:3]

            def step(columns):
                value[:, columns] = (mine[:, columns] + arrived[:, columns]) * slope[:, columns]

            loop(feats, wide, step)
            copy = pltpu.make_async_copy(value, outs[0].at[0, pl.ds(lo, n)], sem)
            copy.start()
            copy.wait()

        ins = [(store[i][k], vector) for k in ("own", "in", "slope")]
        aliases = {}
        if "grad" in saved:
            aliases = {len(ins): 0}
            ins.append((saved["grad"], hbm))
        (saved["grad"],) = chain(
            "finish",
            body,
            ins,
            [(shape((1, share, feats)), hbm)],
            scratch=[pltpu.VMEM((n, feats), f32), pltpu.SemaphoreType.DMA],
            aliases=aliases,
        )

    def decoder_grad():
        def body(ins, outs):
            a, e = ins
            value = three(a[0], a[1], e[0], e[1], across_rows)
            outs[0][0, 0] = value[:, :model]
            outs[0][0, 1] = value[:, model:]

        (out,) = chain(
            "decoder_grad",
            body,
            [
                (saved["acts"], pl.BlockSpec((2, tokens, tile), lambda j: (0, 0, j))),
                (saved["errors"], pl.BlockSpec((2, tokens, 2 * model), lambda j: (0, 0, 0))),
            ],
            [(shape((1, 2, feats, model)), pl.BlockSpec((1, 2, tile, model), lambda j: (0, 0, j, 0)))],
            grid=(feats // tile,),
        )
        return out

    last = len(pieces)

    def at(f, i):
        if 0 <= i < last:
            f(i)

    enter(0)
    summed(0)
    split_decoder()
    at(part, 1)
    goals()
    at(summed, 1)
    for i in range(last + 1):
        at(gate, i)
        at(part, i + 2)
        at(recon, i)
        at(across, i - 1)
        at(summed, i + 2)
        if i == last - 1:
            at(finish, 0)
        at(held, i)
        at(back, i - 1)
        at(middle, i)
        at(turn, i - 1)
        if i == last - 1:
            at(finish, 1)
    dec_grad = decoder_grad()
    for i in range(2, last):
        finish(i)
    return dec_grad, saved["grad"]


def solution(mesh):
    in_specs = (
        P("layer", None, "width"),
        P(None, ("layer", "feat"), "width"),
        P("layer", "width", "feat"),
        P("layer", "feat"),
        P("layer", "feat"),
        P("layer", None, "feat", "width"),
        P(None, "width"),
    )
    out_specs = (P("layer", None, "feat", "width"), P("layer", "width", "feat"))
    return jax.shard_map(local, mesh=mesh, in_specs=in_specs, out_specs=out_specs, check_vma=False)
```

```python
import functools

import jax
import jax.numpy as jnp
from jax import lax
from jax.experimental import pallas as pl
from jax.experimental.pallas import tpu as pltpu
from jax.sharding import PartitionSpec as P

softness = 0.5
eighths = (1, 2, 2, 2, 1)
cuts = 4
f32 = jnp.float32
bf16 = jnp.bfloat16
anywhere = pl.BlockSpec(memory_space=pl.ANY)
scalars = pl.BlockSpec(memory_space=pltpu.SMEM)
vector = pl.BlockSpec(memory_space=pltpu.VMEM)
hbm = pl.BlockSpec(memory_space=pltpu.HBM)
mega = 1024 * 1024


def pieces_of(rows):
    if rows % 128:
        return [(0, rows)]
    bounds = [0]
    for part in eighths:
        bounds.append(bounds[-1] + part * rows // 8)
    return list(zip(bounds[:-1], bounds[1:]))


def halves(value):
    high = value.astype(bf16)
    return high, (value - high.astype(f32)).astype(bf16)


def three(a_high, a_low, b_high, b_low, dims):
    dot = functools.partial(
        lax.dot_general, dimension_numbers=(dims, ((), ())), preferred_element_type=f32
    )
    return dot(a_high, b_high) + (dot(a_low, b_high) + dot(a_high, b_low))


plain = ((1,), (0,))
across_rows = ((0,), (0,))
across_columns = ((1,), (1,))


def shape(dims, kind=f32):
    return jax.ShapeDtypeStruct(dims, kind)


def loop(total, step, body):
    def turn(k, carry):
        body(pl.ds(pl.multiple_of(k * step, step), step))
        return carry

    lax.fori_loop(0, total // step, turn, 0)


def join(refs, columns):
    return jnp.concatenate([r[:, columns] for r in refs])


class Chain:
    def __init__(self):
        self.last = None

    def __call__(
        self, name, body, inputs, outputs, scratch=(), aliases=None, limit=16, grid=None
    ):
        arrays = [a for a, _ in inputs]
        in_specs = [s for _, s in inputs]
        extra = 0
        if self.last is not None:
            arrays.append(self.last)
            in_specs.append(anywhere)
            extra = 1
        count = len(inputs)
        given = len(outputs)

        def kernel(*refs):
            ins = refs[:count]
            outs = refs[count + extra : count + extra + given]
            mark = refs[count + extra + given]
            mark[...] = jnp.zeros_like(mark)
            body(ins, outs, *refs[count + extra + given + 1 :])

        mark_spec = vector if grid is None else pl.BlockSpec((8, 128), lambda *i: (0, 0))
        result = pl.pallas_call(
            kernel,
            grid=grid or (),
            in_specs=in_specs,
            out_specs=[s for _, s in outputs] + [mark_spec],
            out_shape=[o for o, _ in outputs] + [shape((8, 128))],
            scratch_shapes=list(scratch),
            input_output_aliases=aliases or {},
            compiler_params=pltpu.CompilerParams(vmem_limit_bytes=limit * mega),
            cost_estimate=pl.CostEstimate(flops=0, bytes_accessed=0, transcendentals=0),
            name=name,
        )(*arrays)
        self.last = result[-1]
        return result[:-1]


def stream(count, copy, body):
    copy(0).start()
    for k in range(count):
        if k + 1 < count:
            copy(k + 1).start()
        copy(k).wait()
        body(k, k % 2)


def local(inputs, targets, w_enc, b_enc, thresholds, w_dec, b_dec):
    layer_pos = lax.axis_index("layer")
    first = layer_pos == 0
    feat_pos = lax.axis_index("feat")
    feat_size = lax.axis_size("feat")
    width = lax.axis_size("width")
    pos = lax.axis_index("width")
    near = pos % 2
    far = pos // 2
    tokens = inputs.shape[1]
    model = inputs.shape[2]
    feats = w_enc.shape[2]
    share = tokens // width
    tile = min(512, feats)
    tiles = feats // tile
    wide = min(1024, feats)
    near_pairs = [(i, i ^ 1) for i in range(width)]
    far_pairs = [(i, i ^ 2) for i in range(width)]
    pieces = pieces_of(share)
    flags = jnp.stack([first.astype(jnp.int32), far.astype(jnp.int32)])

    def swap_near(arrays):
        return [lax.ppermute(a, "width", near_pairs) for a in arrays]

    def swap_far(a):
        return lax.ppermute(a, "width", far_pairs)

    def arrange(rows):
        split = rows.reshape(2, 2, share, rows.shape[-1])
        found = []
        for lo, hi in pieces:
            cut = split[:, :, lo:hi]
            own = lax.dynamic_index_in_dim(cut, near, 1, keepdims=False)
            other = lax.dynamic_index_in_dim(cut, 1 - near, 1, keepdims=False)
            found.append(jnp.stack([own, other]).reshape(-1, model))
        return found

    x_rows = arrange(inputs[0])
    chain = Chain()
    store = [{} for _ in pieces]
    weights = {}
    saved = {}

    def size(i):
        return pieces[i][1] - pieces[i][0]

    def cut_rows(i):
        return 2 * size(i) // cuts

    def cut_shapes(i):
        return [(shape((cut_rows(i), feats)), vector)] * cuts

    def write_cuts(i, value, own, others, columns):
        n = size(i)
        own[:, columns] = value[: 2 * n]
        for k, out in enumerate(others):
            start = 2 * n + k * cut_rows(i)
            out[:, columns] = value[start : start + cut_rows(i)]

    def enter(i):
        n = size(i)

        def body(ins, outs, buffers, sems):
            x, w = ins
            own, *others, high, low = outs
            x_high, x_low = halves(x[...])

            def read(k):
                return pltpu.make_async_copy(
                    w.at[0, :, pl.ds(k * tile, tile)], buffers.at[k % 2], sems.at[k % 2]
                )

            def step(k, slot):
                columns = slice(k * tile, (k + 1) * tile)
                w_high, w_low = halves(buffers[slot])
                high[:, columns], low[:, columns] = w_high, w_low
                write_cuts(i, three(x_high, x_low, w_high, w_low, plain), own, others, columns)

            stream(tiles, read, step)

        own, *others, high, low = chain(
            "enter",
            body,
            [(x_rows[i], vector), (w_enc, hbm)],
            [(shape((2 * n, feats)), vector)]
            + cut_shapes(i)
            + [(shape((model, feats), bf16), vector)] * 2,
            scratch=[pltpu.VMEM((2, model, tile), f32), pltpu.SemaphoreType.DMA((2,))],
            limit=46,
        )
        weights["enc"] = [high, low]
        store[i]["own"], store[i]["in"] = own, swap_near(others)

    def part(i):
        n = size(i)

        def body(ins, outs):
            x, high, low = ins
            own, *others = outs
            x_high, x_low = halves(x[...])

            def step(columns):
                value = three(x_high, x_low, high[:, columns], low[:, columns], plain)
                write_cuts(i, value, own, others, columns)

            loop(feats, wide, step)

        own, *others = chain(
            "part",
            body,
            [(x_rows[i], vector)] + [(w, vector) for w in weights["enc"]],
            [(shape((2 * n, feats)), vector)] + cut_shapes(i),
        )
        store[i]["own"], store[i]["in"] = own, swap_near(others)

    def summed(i):
        n = size(i)

        def body(ins, outs):
            own, *others = ins

            def step(columns):
                outs[0][:, columns] = own[:, columns] + join(others, columns)

            loop(feats, wide, step)

        (value,) = chain(
            "chip_sum",
            body,
            [(a, vector) for a in [store[i]["own"], *store[i]["in"]]],
            [(shape((2 * n, feats)), vector)],
        )
        store[i]["sum"], store[i]["in"] = value, swap_far(value)

    def split_decoder():
        def body(ins, outs, buffers, sems):
            w = ins[0]
            high, low = outs

            def read(k):
                return pltpu.make_async_copy(
                    w.at[0, :, pl.ds(k * tile, tile)], buffers.at[k % 2], sems.at[k % 2]
                )

            def step(k, slot):
                rows = slice(k * tile, (k + 1) * tile)
                for t in range(2):
                    high[t, rows], low[t, rows] = halves(buffers[slot, t])

            stream(tiles, read, step)

        weights["dec"] = chain(
            "split_decoder",
            body,
            [(w_dec, hbm)],
            [(shape((2, feats, model), bf16), vector)] * 2,
            scratch=[pltpu.VMEM((2, 2, tile, model), f32), pltpu.SemaphoreType.DMA((2,))],
            limit=28,
        )

    def goals():
        share_rows = targets.shape[1]

        def body(ins, outs):
            flag, goal = ins
            home, away = outs
            own = flag[0] == 1
            home[...] = jnp.where(own, goal[0], goal[1])
            away[...] = jnp.where(own, goal[1], goal[0])

        home, away = chain(
            "targets",
            body,
            [(flags, scalars), (targets, vector)],
            [(shape((share_rows, model)), vector)] * 2,
        )
        away = lax.ppermute(away, "layer", [(0, 1), (1, 0)])
        padded = jnp.zeros((tokens, model), f32)
        home_start = (layer_pos * feat_size + feat_pos) * share_rows
        away_start = ((1 - layer_pos) * feat_size + feat_pos) * share_rows
        padded = lax.dynamic_update_slice(padded, home, (home_start, jnp.int32(0)))
        padded = lax.dynamic_update_slice(padded, away, (away_start, jnp.int32(0)))
        weights["goal"] = arrange(padded)

    def gate(i):
        n = size(i)

        def body(ins, outs):
            flag, s, r, b, th = ins
            *acts, slope = outs

            def step(columns):
                bias, edge = b[:, columns], th[:, columns]

                def opened(pre):
                    return jax.nn.sigmoid((pre - edge) / softness)

                for k, out in enumerate(acts):
                    rows = slice(k * cut_rows(i), (k + 1) * cut_rows(i))
                    pre = s[rows, columns] + r[rows, columns] + bias
                    out[:, columns] = pre * opened(pre)
                rows = pl.ds(pl.multiple_of(flag[1] * n, n), n)
                pre = s[rows, columns] + r[rows, columns] + bias
                own = opened(pre)
                slope[:, columns] = own + pre * own * (1.0 - own) / softness

            loop(feats, wide, step)

        *acts, slope = chain(
            "gate",
            body,
            [
                (flags, scalars),
                (store[i]["sum"], vector),
                (store[i]["in"], vector),
                (b_enc, vector),
                (thresholds, vector),
            ],
            cut_shapes(i) + [(shape((n, feats)), vector)],
        )
        store[i]["acts"], store[i]["slope"], store[i]["in"] = acts, slope, swap_near(acts)

    def recon(i):
        n = size(i)
        lo = pieces[i][0]

        def body(ins, outs, made, sem):
            own, other = ins[:cuts], ins[cuts : 2 * cuts]
            high, low = ins[2 * cuts : 2 * cuts + 2]
            r0, r1, kept = outs
            rows = pl.ds(4 * lo, 4 * n)
            r0[...] = jnp.zeros_like(r0)
            r1[...] = jnp.zeros_like(r1)

            def step(columns):
                a_high, a_low = halves(join(own + other, columns))
                made[0, :, columns], made[1, :, columns] = a_high, a_low
                pltpu.make_async_copy(
                    made.at[:, :, columns], kept.at[pl.ds(0, 2), rows, columns], sem
                ).start()
                for t, out in enumerate((r0, r1)):
                    out[...] += three(a_high, a_low, high[t, columns], low[t, columns], plain)

            loop(feats, wide, step)
            pltpu.make_async_copy(made, kept.at[pl.ds(0, 2), rows], sem).wait()

        ins = [(a, vector) for a in [*store[i]["acts"], *store[i]["in"], *weights["dec"]]]
        outs = [(shape((4 * n, model)), vector)] * 2
        aliases = {}
        if "acts" in saved:
            aliases = {len(ins): len(outs)}
            ins.append((saved["acts"], hbm))
        outs.append((shape((4, tokens, feats), bf16), hbm))
        r0, r1, saved["acts"] = chain(
            "recon",
            body,
            ins,
            outs,
            scratch=[pltpu.VMEM((2, 4 * n, feats), bf16), pltpu.SemaphoreType.DMA],
            aliases=aliases,
        )
        store[i]["r"] = (r0, r1)
        store[i]["in"] = lax.ppermute(r1, "layer", [(0, 1)])

    def held(i):
        n = size(i)

        def body(ins, outs):
            flag, r0, r1, below, goal = ins
            outs[0][...] = jnp.where(flag[0] == 1, r0[...], r1[...] + below[...]) - goal[...]

        arrays = [*store[i]["r"], store[i]["in"], weights["goal"][i]]
        (value,) = chain(
            "held",
            body,
            [(flags, scalars)] + [(a, vector) for a in arrays],
            [(shape((4 * n, model)), vector)],
        )
        store[i]["held"] = value
        if feat_size <= 4:
            store[i]["in"] = lax.ppermute(value, "feat", [(k, k ^ 1) for k in range(feat_size)])
        else:
            store[i]["in"] = lax.psum(value, "feat")
            store[i]["held"] = jnp.zeros_like(value)

    def middle(i):
        n = size(i)
        if feat_size > 4:
            return

        def body(ins, outs):
            outs[0][...] = ins[0][...] + ins[1][...]

        (value,) = chain(
            "feat_sum",
            body,
            [(store[i]["held"], vector), (store[i]["in"], vector)],
            [(shape((4 * n, model)), vector)],
        )
        store[i]["held"] = value
        store[i]["in"] = lax.ppermute(value, "feat", [(k, k ^ 2) for k in range(feat_size)])

    def across(i):
        n = size(i)

        def body(ins, outs):
            flag, a, b, bias = ins
            line = jnp.where(flag[0] == 1, bias[0:1, :], bias[1:2, :])
            outs[0][...] = a[...] + b[...] + line

        (value,) = chain(
            "errors",
            body,
            [(flags, scalars)] + [(a, vector) for a in (store[i]["held"], store[i]["in"], b_dec)],
            [(shape((4 * n, model)), vector)],
        )
        store[i]["held"] = value
        store[i]["in"] = lax.ppermute(value, "layer", [(1, 0)])

    def back(i):
        n = size(i)

        def body(ins, outs):
            flag, value, above, high, low = ins
            own, *others, e = outs
            e_high, e_low = e.at[0], e.at[1]
            is_first = flag[0] == 1
            zero = jnp.where(is_first, value[...], 0.0)
            one = jnp.where(is_first, above[...], value[...])
            e_high[:, :model], e_low[:, :model] = halves(zero)
            e_high[:, model:], e_low[:, model:] = halves(one)
            def step(columns):
                total = None
                for t in range(2):
                    cut = slice(t * model, (t + 1) * model)
                    term = three(
                        e_high[:, cut], e_low[:, cut], high[t, columns], low[t, columns], across_columns
                    )
                    total = term if total is None else total + term
                write_cuts(i, total, own, others, columns)

            loop(feats, wide, step)

        arrays = [store[i]["held"], store[i]["in"], *weights["dec"]]
        ins = [(flags, scalars)] + [(a, vector) for a in arrays]
        outs = [(shape((2 * n, feats)), vector)] + cut_shapes(i)
        outs.append((shape((2, 4 * n, 2 * model), bf16), vector))
        own, *others, store[i]["errors"] = chain("back", body, ins, outs)
        store[i]["own"], store[i]["in"] = own, swap_near(others)

    def turn(i):
        n = size(i)
        half = cuts // 2

        def body(ins, outs):
            flag, own, *others = ins
            mine, theirs = outs
            for place in range(2):

                @pl.when(flag[1] == place)
                def _():
                    for out, at in ((mine, place), (theirs, 1 - place)):

                        def step(columns):
                            arrived = join(others[at * half : (at + 1) * half], columns)
                            out[:, columns] = own[at * n : (at + 1) * n, columns] + arrived

                        loop(feats, wide, step)

        mine, theirs = chain(
            "turn",
            body,
            [(flags, scalars)] + [(a, vector) for a in [store[i]["own"], *store[i]["in"]]],
            [(shape((n, feats)), vector)] * 2,
        )
        store[i]["own"], store[i]["in"] = mine, swap_far(theirs)

    def finish(i):
        lo, hi = pieces[i]
        n = size(i)

        def body(ins, outs, value, sem):
            mine, arrived, slope = ins[:3]

            def step(columns):
                value[:, columns] = (mine[:, columns] + arrived[:, columns]) * slope[:, columns]

            loop(feats, wide, step)
            copy = pltpu.make_async_copy(value, outs[0].at[0, pl.ds(lo, n)], sem)
            copy.start()
            copy.wait()

        ins = [(store[i][k], vector) for k in ("own", "in", "slope")]
        aliases = {}
        if "grad" in saved:
            aliases = {len(ins): 0}
            ins.append((saved["grad"], hbm))
        (saved["grad"],) = chain(
            "finish",
            body,
            ins,
            [(shape((1, share, feats)), hbm)],
            scratch=[pltpu.VMEM((n, feats), f32), pltpu.SemaphoreType.DMA],
            aliases=aliases,
        )

    def decoder_grad():
        def body(ins, outs, e):
            a, *errors = ins

            @pl.when(pl.program_id(0) == 0)
            def _():
                for (lo, hi), piece in zip(pieces, errors):
                    e[:, 4 * lo : 4 * hi] = piece[...]

            value = three(a[0], a[1], e[0], e[1], across_rows)
            outs[0][0, 0] = value[:, :model]
            outs[0][0, 1] = value[:, model:]

        errors = [s["errors"] for s in store]
        (out,) = chain(
            "decoder_grad",
            body,
            [(saved["acts"], pl.BlockSpec((2, tokens, tile), lambda j: (0, 0, j)))]
            + [(e, pl.BlockSpec(e.shape, lambda j: (0, 0, 0))) for e in errors],
            [(shape((1, 2, feats, model)), pl.BlockSpec((1, 2, tile, model), lambda j: (0, 0, j, 0)))],
            scratch=[pltpu.VMEM((2, tokens, 2 * model), bf16)],
            limit=46,
            grid=(tiles,),
        )
        return out

    last = len(pieces)

    def at(f, i):
        if 0 <= i < last:
            f(i)

    enter(0)
    at(part, 1)
    summed(0)
    split_decoder()
    at(summed, 1)
    for i in range(last + 2):
        if i:
            at(summed, i + 1)
        at(turn, i - 3)
        at(gate, i)
        if i == 0:
            goals()
        at(across, i - 2)
        at(held, i - 1)
        at(part, i + 2)
        at(recon, i)
        at(middle, i - 1)
        at(back, i - 2)
        if i >= last - 1:
            at(finish, i - last + 1)
    turn(last - 1)
    dec_grad = decoder_grad()
    for i in range(3, last):
        finish(i)
    return dec_grad, saved["grad"]


def solution(mesh):
    in_specs = (
        P("layer", None, "width"),
        P(None, ("layer", "feat"), "width"),
        P("layer", "width", "feat"),
        P("layer", "feat"),
        P("layer", "feat"),
        P("layer", None, "feat", "width"),
        P(None, "width"),
    )
    out_specs = (P("layer", None, "feat", "width"), P("layer", "width", "feat"))
    return jax.shard_map(local, mesh=mesh, in_specs=in_specs, out_specs=out_specs, check_vma=False)
```

```python
import functools

import jax
import jax.numpy as jnp
from jax import lax
from jax.experimental import pallas as pl
from jax.experimental.pallas import tpu as pltpu
from jax.sharding import PartitionSpec as P

softness = 0.5
eighths = (1, 2, 2, 2, 1)
cuts = 4
order = (
    ("enter", 0), ("goals", 0), ("sum", 0), ("part", 3), ("split", 0), ("part", 1), ("sum", 3),
    ("part", 2), ("part", 4), ("gate", 0), ("recon", 0), ("sum", 1), ("held", 0), ("sum", 2),
    ("mid", 0), ("gate", 3), ("err", 0), ("recon", 3), ("sum", 4), ("back", 0), ("held", 3),
    ("gate", 1), ("mid", 3), ("recon", 1), ("turn", 0), ("err", 3), ("held", 1), ("gate", 2),
    ("back", 3), ("mid", 1), ("recon", 2), ("gate", 4), ("turn", 3), ("held", 2), ("recon", 4),
    ("err", 1), ("held", 4), ("mid", 2), ("back", 1), ("mid", 4), ("err", 2), ("turn", 1),
    ("fin", 3), ("fin", 0), ("err", 4), ("back", 2), ("back", 4), ("turn", 2), ("dg", 0),
    ("fin", 1), ("turn", 4), ("dg", 1), ("fin", 4), ("fin", 2),
)
f32 = jnp.float32
bf16 = jnp.bfloat16
anywhere = pl.BlockSpec(memory_space=pl.ANY)
scalars = pl.BlockSpec(memory_space=pltpu.SMEM)
vector = pl.BlockSpec(memory_space=pltpu.VMEM)
hbm = pl.BlockSpec(memory_space=pltpu.HBM)
mega = 1024 * 1024


def pieces_of(rows):
    if rows % 128:
        return [(0, rows)]
    bounds = [0]
    for part in eighths:
        bounds.append(bounds[-1] + part * rows // 8)
    return list(zip(bounds[:-1], bounds[1:]))


def plain_order(count):
    found = [("enter", 0), ("split", 0), ("goals", 0)]
    for i in range(count):
        for stage in ("part", "sum", "gate", "recon", "held", "mid", "err", "back", "turn", "fin"):
            if i or stage != "part":
                found.append((stage, i))
    return found + [("dg", step) for step in range(min(count, 2))]


def halves(value):
    high = value.astype(bf16)
    return high, (value - high.astype(f32)).astype(bf16)


def three(a_high, a_low, b_high, b_low, dims):
    dot = functools.partial(
        lax.dot_general, dimension_numbers=(dims, ((), ())), preferred_element_type=f32
    )
    return dot(a_high, b_high) + (dot(a_low, b_high) + dot(a_high, b_low))


plain = ((1,), (0,))
across_rows = ((0,), (0,))
across_columns = ((1,), (1,))


def shape(dims, kind=f32):
    return jax.ShapeDtypeStruct(dims, kind)


def loop(total, step, body):
    def turn(k, carry):
        body(pl.ds(pl.multiple_of(k * step, step), step))
        return carry

    lax.fori_loop(0, total // step, turn, 0)


def join(refs, columns):
    return jnp.concatenate([r[:, columns] for r in refs])


class Chain:
    def __init__(self):
        self.last = None

    def __call__(
        self, name, body, inputs, outputs, scratch=(), aliases=None, limit=16, grid=None
    ):
        arrays = [a for a, _ in inputs]
        in_specs = [s for _, s in inputs]
        extra = 0
        if self.last is not None:
            arrays.append(self.last)
            in_specs.append(anywhere)
            extra = 1
        count = len(inputs)
        given = len(outputs)

        def kernel(*refs):
            ins = refs[:count]
            outs = refs[count + extra : count + extra + given]
            mark = refs[count + extra + given]
            mark[...] = jnp.zeros_like(mark)
            body(ins, outs, *refs[count + extra + given + 1 :])

        mark_spec = vector if grid is None else pl.BlockSpec((8, 128), lambda *i: (0, 0))
        result = pl.pallas_call(
            kernel,
            grid=grid or (),
            in_specs=in_specs,
            out_specs=[s for _, s in outputs] + [mark_spec],
            out_shape=[o for o, _ in outputs] + [shape((8, 128))],
            scratch_shapes=list(scratch),
            input_output_aliases=aliases or {},
            compiler_params=pltpu.CompilerParams(vmem_limit_bytes=limit * mega),
            cost_estimate=pl.CostEstimate(flops=0, bytes_accessed=0, transcendentals=0),
            name=name,
        )(*arrays)
        self.last = result[-1]
        return result[:-1]


def stream(count, copy, body):
    copy(0).start()
    for k in range(count):
        if k + 1 < count:
            copy(k + 1).start()
        copy(k).wait()
        body(k, k % 2)


def local(inputs, targets, w_enc, b_enc, thresholds, w_dec, b_dec):
    layer_pos = lax.axis_index("layer")
    first = layer_pos == 0
    feat_pos = lax.axis_index("feat")
    feat_size = lax.axis_size("feat")
    width = lax.axis_size("width")
    pos = lax.axis_index("width")
    near = pos % 2
    far = pos // 2
    tokens = inputs.shape[1]
    model = inputs.shape[2]
    feats = w_enc.shape[2]
    share = tokens // width
    tile = min(512, feats)
    tiles = feats // tile
    wide = min(1024, feats)
    near_pairs = [(i, i ^ 1) for i in range(width)]
    far_pairs = [(i, i ^ 2) for i in range(width)]
    pieces = pieces_of(share)
    flags = jnp.stack([first.astype(jnp.int32), far.astype(jnp.int32)])

    def swap_near(arrays):
        return [lax.ppermute(a, "width", near_pairs) for a in arrays]

    def swap_far(a):
        return lax.ppermute(a, "width", far_pairs)

    def arrange(rows):
        split = rows.reshape(2, 2, share, rows.shape[-1])
        found = []
        for lo, hi in pieces:
            cut = split[:, :, lo:hi]
            own = lax.dynamic_index_in_dim(cut, near, 1, keepdims=False)
            other = lax.dynamic_index_in_dim(cut, 1 - near, 1, keepdims=False)
            found.append(jnp.stack([own, other]).reshape(-1, model))
        return found

    x_rows = arrange(inputs[0])
    chain = Chain()
    store = [{} for _ in pieces]
    weights = {}
    saved = {}

    def size(i):
        return pieces[i][1] - pieces[i][0]

    def cut_rows(i):
        return 2 * size(i) // cuts

    def cut_shapes(i):
        return [(shape((cut_rows(i), feats)), vector)] * cuts

    def write_cuts(i, value, own, others, columns):
        n = size(i)
        own[:, columns] = value[: 2 * n]
        for k, out in enumerate(others):
            start = 2 * n + k * cut_rows(i)
            out[:, columns] = value[start : start + cut_rows(i)]

    def enter(i):
        n = size(i)

        def body(ins, outs, buffers, sems):
            x, w = ins
            own, *others, high, low = outs
            x_high, x_low = halves(x[...])

            def read(k):
                return pltpu.make_async_copy(
                    w.at[0, :, pl.ds(k * tile, tile)], buffers.at[k % 2], sems.at[k % 2]
                )

            def step(k, slot):
                columns = slice(k * tile, (k + 1) * tile)
                w_high, w_low = halves(buffers[slot])
                high[:, columns], low[:, columns] = w_high, w_low
                write_cuts(i, three(x_high, x_low, w_high, w_low, plain), own, others, columns)

            stream(tiles, read, step)

        own, *others, high, low = chain(
            "enter",
            body,
            [(x_rows[i], vector), (w_enc, hbm)],
            [(shape((2 * n, feats)), vector)]
            + cut_shapes(i)
            + [(shape((model, feats), bf16), vector)] * 2,
            scratch=[pltpu.VMEM((2, model, tile), f32), pltpu.SemaphoreType.DMA((2,))],
            limit=46,
        )
        weights["enc"] = [high, low]
        store[i]["own"], store[i]["in"] = own, swap_near(others)

    def part(i):
        n = size(i)

        def body(ins, outs):
            x, high, low = ins
            own, *others = outs
            x_high, x_low = halves(x[...])

            def step(columns):
                value = three(x_high, x_low, high[:, columns], low[:, columns], plain)
                write_cuts(i, value, own, others, columns)

            loop(feats, wide, step)

        own, *others = chain(
            "part",
            body,
            [(x_rows[i], vector)] + [(w, vector) for w in weights["enc"]],
            [(shape((2 * n, feats)), vector)] + cut_shapes(i),
        )
        store[i]["own"], store[i]["in"] = own, swap_near(others)

    def summed(i):
        n = size(i)

        def body(ins, outs):
            own, *others = ins

            def step(columns):
                outs[0][:, columns] = own[:, columns] + join(others, columns)

            loop(feats, wide, step)

        (value,) = chain(
            "chip_sum",
            body,
            [(a, vector) for a in [store[i]["own"], *store[i]["in"]]],
            [(shape((2 * n, feats)), vector)],
        )
        store[i]["sum"], store[i]["in"] = value, swap_far(value)

    def split_decoder(_):
        def body(ins, outs, buffers, sems):
            w = ins[0]
            high, low = outs

            def read(k):
                return pltpu.make_async_copy(
                    w.at[0, :, pl.ds(k * tile, tile)], buffers.at[k % 2], sems.at[k % 2]
                )

            def step(k, slot):
                rows = slice(k * tile, (k + 1) * tile)
                for t in range(2):
                    high[t, rows], low[t, rows] = halves(buffers[slot, t])

            stream(tiles, read, step)

        weights["dec"] = chain(
            "split_decoder",
            body,
            [(w_dec, hbm)],
            [(shape((2, feats, model), bf16), vector)] * 2,
            scratch=[pltpu.VMEM((2, 2, tile, model), f32), pltpu.SemaphoreType.DMA((2,))],
            limit=28,
        )

    def goals(_):
        share_rows = targets.shape[1]

        def body(ins, outs):
            flag, goal = ins
            home, away = outs
            own = flag[0] == 1
            home[...] = jnp.where(own, goal[0], goal[1])
            away[...] = jnp.where(own, goal[1], goal[0])

        home, away = chain(
            "targets",
            body,
            [(flags, scalars), (targets, vector)],
            [(shape((share_rows, model)), vector)] * 2,
        )
        away = lax.ppermute(away, "layer", [(0, 1), (1, 0)])
        padded = jnp.zeros((tokens, model), f32)
        home_start = (layer_pos * feat_size + feat_pos) * share_rows
        away_start = ((1 - layer_pos) * feat_size + feat_pos) * share_rows
        padded = lax.dynamic_update_slice(padded, home, (home_start, jnp.int32(0)))
        padded = lax.dynamic_update_slice(padded, away, (away_start, jnp.int32(0)))
        weights["goal"] = arrange(padded)

    def gate(i):
        n = size(i)

        def body(ins, outs):
            flag, s, r, b, th = ins
            *acts, slope = outs

            def step(columns):
                bias, edge = b[:, columns], th[:, columns]

                def opened(pre):
                    return jax.nn.sigmoid((pre - edge) / softness)

                for k, out in enumerate(acts):
                    rows = slice(k * cut_rows(i), (k + 1) * cut_rows(i))
                    pre = s[rows, columns] + r[rows, columns] + bias
                    out[:, columns] = pre * opened(pre)
                rows = pl.ds(pl.multiple_of(flag[1] * n, n), n)
                pre = s[rows, columns] + r[rows, columns] + bias
                own = opened(pre)
                slope[:, columns] = own + pre * own * (1.0 - own) / softness

            loop(feats, wide, step)

        *acts, slope = chain(
            "gate",
            body,
            [
                (flags, scalars),
                (store[i]["sum"], vector),
                (store[i]["in"], vector),
                (b_enc, vector),
                (thresholds, vector),
            ],
            cut_shapes(i) + [(shape((n, feats)), vector)],
        )
        store[i]["acts"], store[i]["slope"], store[i]["in"] = acts, slope, swap_near(acts)

    def recon(i):
        n = size(i)
        lo = pieces[i][0]

        def body(ins, outs, made, sem):
            own, other = ins[:cuts], ins[cuts : 2 * cuts]
            high, low = ins[2 * cuts : 2 * cuts + 2]
            r0, r1, kept = outs
            rows = pl.ds(4 * lo, 4 * n)
            r0[...] = jnp.zeros_like(r0)
            r1[...] = jnp.zeros_like(r1)

            def step(columns):
                a_high, a_low = halves(join(own + other, columns))
                made[0, :, columns], made[1, :, columns] = a_high, a_low
                pltpu.make_async_copy(
                    made.at[:, :, columns], kept.at[pl.ds(0, 2), rows, columns], sem
                ).start()
                for t, out in enumerate((r0, r1)):
                    out[...] += three(a_high, a_low, high[t, columns], low[t, columns], plain)

            loop(feats, wide, step)
            pltpu.make_async_copy(made, kept.at[pl.ds(0, 2), rows], sem).wait()

        ins = [(a, vector) for a in [*store[i]["acts"], *store[i]["in"], *weights["dec"]]]
        outs = [(shape((4 * n, model)), vector)] * 2
        aliases = {}
        if "acts" in saved:
            aliases = {len(ins): len(outs)}
            ins.append((saved["acts"], hbm))
        outs.append((shape((4, tokens, feats), bf16), hbm))
        r0, r1, saved["acts"] = chain(
            "recon",
            body,
            ins,
            outs,
            scratch=[pltpu.VMEM((2, 4 * n, feats), bf16), pltpu.SemaphoreType.DMA],
            aliases=aliases,
        )
        store[i]["r"] = (r0, r1)
        store[i]["in"] = lax.ppermute(r1, "layer", [(0, 1)])

    def held(i):
        n = size(i)

        def body(ins, outs):
            flag, r0, r1, below, goal = ins
            outs[0][...] = jnp.where(flag[0] == 1, r0[...], r1[...] + below[...]) - goal[...]

        arrays = [*store[i]["r"], store[i]["in"], weights["goal"][i]]
        (value,) = chain(
            "held",
            body,
            [(flags, scalars)] + [(a, vector) for a in arrays],
            [(shape((4 * n, model)), vector)],
        )
        store[i]["held"] = value
        if feat_size <= 4:
            store[i]["in"] = lax.ppermute(value, "feat", [(k, k ^ 1) for k in range(feat_size)])
        else:
            store[i]["in"] = lax.psum(value, "feat")
            store[i]["held"] = jnp.zeros_like(value)

    def middle(i):
        n = size(i)
        if feat_size > 4:
            return

        def body(ins, outs):
            outs[0][...] = ins[0][...] + ins[1][...]

        (value,) = chain(
            "feat_sum",
            body,
            [(store[i]["held"], vector), (store[i]["in"], vector)],
            [(shape((4 * n, model)), vector)],
        )
        store[i]["held"] = value
        store[i]["in"] = lax.ppermute(value, "feat", [(k, k ^ 2) for k in range(feat_size)])

    def across(i):
        n = size(i)

        def body(ins, outs):
            flag, a, b, bias = ins
            line = jnp.where(flag[0] == 1, bias[0:1, :], bias[1:2, :])
            outs[0][...] = a[...] + b[...] + line

        (value,) = chain(
            "errors",
            body,
            [(flags, scalars)] + [(a, vector) for a in (store[i]["held"], store[i]["in"], b_dec)],
            [(shape((4 * n, model)), vector)],
        )
        store[i]["held"] = value
        store[i]["in"] = lax.ppermute(value, "layer", [(1, 0)])

    def back(i):
        n = size(i)

        def body(ins, outs):
            flag, value, above, high, low = ins
            own, *others, e = outs
            e_high, e_low = e.at[0], e.at[1]
            is_first = flag[0] == 1
            zero = jnp.where(is_first, value[...], 0.0)
            one = jnp.where(is_first, above[...], value[...])
            e_high[:, :model], e_low[:, :model] = halves(zero)
            e_high[:, model:], e_low[:, model:] = halves(one)
            def step(columns):
                total = None
                for t in range(2):
                    cut = slice(t * model, (t + 1) * model)
                    term = three(
                        e_high[:, cut], e_low[:, cut], high[t, columns], low[t, columns], across_columns
                    )
                    total = term if total is None else total + term
                write_cuts(i, total, own, others, columns)

            loop(feats, wide, step)

        arrays = [store[i]["held"], store[i]["in"], *weights["dec"]]
        ins = [(flags, scalars)] + [(a, vector) for a in arrays]
        outs = [(shape((2 * n, feats)), vector)] + cut_shapes(i)
        outs.append((shape((2, 4 * n, 2 * model), bf16), vector))
        own, *others, store[i]["errors"] = chain("back", body, ins, outs)
        store[i]["own"], store[i]["in"] = own, swap_near(others)

    def turn(i):
        n = size(i)
        half = cuts // 2

        def body(ins, outs):
            flag, own, *others = ins
            mine, theirs = outs
            for place in range(2):

                @pl.when(flag[1] == place)
                def _():
                    for out, at in ((mine, place), (theirs, 1 - place)):

                        def step(columns):
                            arrived = join(others[at * half : (at + 1) * half], columns)
                            out[:, columns] = own[at * n : (at + 1) * n, columns] + arrived

                        loop(feats, wide, step)

        mine, theirs = chain(
            "turn",
            body,
            [(flags, scalars)] + [(a, vector) for a in [store[i]["own"], *store[i]["in"]]],
            [(shape((n, feats)), vector)] * 2,
        )
        store[i]["own"], store[i]["in"] = mine, swap_far(theirs)

    def finish(i):
        lo, hi = pieces[i]
        n = size(i)

        def body(ins, outs, value, sem):
            mine, arrived, slope = ins[:3]

            def step(columns):
                value[:, columns] = (mine[:, columns] + arrived[:, columns]) * slope[:, columns]

            loop(feats, wide, step)
            copy = pltpu.make_async_copy(value, outs[0].at[0, pl.ds(lo, n)], sem)
            copy.start()
            copy.wait()

        ins = [(store[i][k], vector) for k in ("own", "in", "slope")]
        aliases = {}
        if "grad" in saved:
            aliases = {len(ins): 0}
            ins.append((saved["grad"], hbm))
        (saved["grad"],) = chain(
            "finish",
            body,
            ins,
            [(shape((1, share, feats)), hbm)],
            scratch=[pltpu.VMEM((n, feats), f32), pltpu.SemaphoreType.DMA],
            aliases=aliases,
        )

    def decoder_grad(step):
        span = pieces[:-1] if step == 0 and len(pieces) > 1 else pieces[-1:]
        base, rows = 4 * span[0][0], 4 * (span[-1][1] - span[0][0])
        assert base % rows == 0

        def body(ins, outs, e):
            a, *errors = ins[: 1 + len(span)]

            @pl.when(pl.program_id(0) == 0)
            def _():
                for (lo, hi), piece in zip(span, errors):
                    e[:, 4 * lo - base : 4 * hi - base] = piece[...]

            value = three(a[0], a[1], e[0], e[1], across_rows)
            for t in range(2):
                part_value = value[:, t * model : (t + 1) * model]
                if step:
                    part_value = part_value + ins[1 + len(span)][0, t]
                outs[0][0, t] = part_value

        errors = [store[pieces.index(p)]["errors"] for p in span]
        out_block = pl.BlockSpec((1, 2, tile, model), lambda j: (0, 0, j, 0))
        ins = [(saved["acts"], pl.BlockSpec((2, rows, tile), lambda j: (0, base // rows, j)))]
        ins += [(e, pl.BlockSpec(e.shape, lambda j: (0, 0, 0))) for e in errors]
        aliases = {}
        if step:
            aliases = {len(ins): 0}
            ins.append((weights["grad"], out_block))
        (weights["grad"],) = chain(
            "decoder_grad",
            body,
            ins,
            [(shape((1, 2, feats, model)), out_block)],
            scratch=[pltpu.VMEM((2, rows, 2 * model), bf16)],
            limit=46,
            aliases=aliases,
            grid=(tiles,),
        )

    last = len(pieces)

    stages = {
        "enter": enter,
        "part": part,
        "sum": summed,
        "split": split_decoder,
        "goals": goals,
        "gate": gate,
        "recon": recon,
        "held": held,
        "mid": middle,
        "err": across,
        "back": back,
        "turn": turn,
        "fin": finish,
        "dg": decoder_grad,
    }
    for stage, i in order if last == len(eighths) else plain_order(last):
        stages[stage](i)
    dec_grad = weights["grad"]
    return dec_grad, saved["grad"]


def solution(mesh):
    in_specs = (
        P("layer", None, "width"),
        P(None, ("layer", "feat"), "width"),
        P("layer", "width", "feat"),
        P("layer", "feat"),
        P("layer", "feat"),
        P("layer", None, "feat", "width"),
        P(None, "width"),
    )
    out_specs = (P("layer", None, "feat", "width"), P("layer", "width", "feat"))
    return jax.shard_map(local, mesh=mesh, in_specs=in_specs, out_specs=out_specs, check_vma=False)
```

```python
import functools

import jax
import jax.numpy as jnp
from jax import lax
from jax.experimental import pallas as pl
from jax.experimental.pallas import tpu as pltpu
from jax.sharding import PartitionSpec as P

softness = 0.5
eighths = (1, 2, 2, 2, 1)
cuts = 4
order = (
    ("enter", 0), ("goals", 0), ("sum", 0), ("part", 3), ("split", 0), ("part", 1), ("sum", 3),
    ("part", 2), ("part", 4), ("gate", 0), ("recon", 0), ("sum", 1), ("held", 0), ("sum", 2),
    ("mid", 0), ("gate", 3), ("err", 0), ("recon", 3), ("sum", 4), ("back", 0), ("held", 3),
    ("gate", 1), ("mid", 3), ("recon", 1), ("turn", 0), ("err", 3), ("held", 1), ("gate", 2),
    ("back", 3), ("mid", 1), ("recon", 2), ("gate", 4), ("turn", 3), ("held", 2), ("recon", 4),
    ("err", 1), ("held", 4), ("mid", 2), ("mid", 4), ("back", 1), ("err", 2), ("turn", 1),
    ("fin", 3), ("fin", 0), ("err", 4), ("back", 2), ("back", 4), ("turn", 2), ("dg", 0),
    ("fin", 1), ("turn", 4), ("dg", 1), ("fin", 4), ("fin", 2),
)
f32 = jnp.float32
bf16 = jnp.bfloat16
anywhere = pl.BlockSpec(memory_space=pl.ANY)
scalars = pl.BlockSpec(memory_space=pltpu.SMEM)
vector = pl.BlockSpec(memory_space=pltpu.VMEM)
hbm = pl.BlockSpec(memory_space=pltpu.HBM)
mega = 1024 * 1024


def pieces_of(rows):
    if rows % 128:
        return [(0, rows)]
    bounds = [0]
    for part in eighths:
        bounds.append(bounds[-1] + part * rows // 8)
    return list(zip(bounds[:-1], bounds[1:]))


def plain_order(count):
    found = [("enter", 0), ("split", 0), ("goals", 0)]
    for i in range(count):
        for stage in ("part", "sum", "gate", "recon", "held", "mid", "err", "back", "turn", "fin"):
            if i or stage != "part":
                found.append((stage, i))
    return found + [("dg", step) for step in range(2) if step or count > 1]


def halves(value):
    high = value.astype(bf16)
    return high, (value - high.astype(f32)).astype(bf16)


def three(a_high, a_low, b_high, b_low, dims):
    dot = functools.partial(
        lax.dot_general, dimension_numbers=(dims, ((), ())), preferred_element_type=f32
    )
    return dot(a_high, b_high) + (dot(a_low, b_high) + dot(a_high, b_low))


plain = ((1,), (0,))
across_rows = ((0,), (0,))
across_columns = ((1,), (1,))


def shape(dims, kind=f32):
    return jax.ShapeDtypeStruct(dims, kind)


def loop(total, step, body):
    def turn(k, carry):
        body(pl.ds(pl.multiple_of(k * step, step), step))
        return carry

    lax.fori_loop(0, total // step, turn, 0)


def join(refs, columns):
    return jnp.concatenate([r[:, columns] for r in refs])


class Chain:
    def __init__(self):
        self.last = None

    def __call__(
        self, name, body, inputs, outputs, scratch=(), aliases=None, limit=16, grid=None
    ):
        arrays = [a for a, _ in inputs]
        in_specs = [s for _, s in inputs]
        extra = 0
        if self.last is not None:
            arrays.append(self.last)
            in_specs.append(anywhere)
            extra = 1
        count = len(inputs)
        given = len(outputs)

        def kernel(*refs):
            ins = refs[:count]
            outs = refs[count + extra : count + extra + given]
            mark = refs[count + extra + given]
            mark[...] = jnp.zeros_like(mark)
            body(ins, outs, *refs[count + extra + given + 1 :])

        mark_spec = vector if grid is None else pl.BlockSpec((8, 128), lambda *i: (0, 0))
        result = pl.pallas_call(
            kernel,
            grid=grid or (),
            in_specs=in_specs,
            out_specs=[s for _, s in outputs] + [mark_spec],
            out_shape=[o for o, _ in outputs] + [shape((8, 128))],
            scratch_shapes=list(scratch),
            input_output_aliases=aliases or {},
            compiler_params=pltpu.CompilerParams(vmem_limit_bytes=limit * mega),
            cost_estimate=pl.CostEstimate(flops=0, bytes_accessed=0, transcendentals=0),
            name=name,
        )(*arrays)
        self.last = result[-1]
        return result[:-1]


def stream(count, copy, body):
    copy(0).start()
    for k in range(count):
        if k + 1 < count:
            copy(k + 1).start()
        copy(k).wait()
        body(k, k % 2)


def local(inputs, targets, w_enc, b_enc, thresholds, w_dec, b_dec):
    layer_pos = lax.axis_index("layer")
    first = layer_pos == 0
    feat_pos = lax.axis_index("feat")
    feat_size = lax.axis_size("feat")
    width = lax.axis_size("width")
    pos = lax.axis_index("width")
    near = pos % 2
    far = pos // 2
    tokens = inputs.shape[1]
    model = inputs.shape[2]
    feats = w_enc.shape[2]
    share = tokens // width
    tile = min(512, feats)
    tiles = feats // tile
    wide = min(1024, feats)
    near_pairs = [(i, i ^ 1) for i in range(width)]
    far_pairs = [(i, i ^ 2) for i in range(width)]
    pieces = pieces_of(share)
    flags = jnp.stack([first.astype(jnp.int32), far.astype(jnp.int32)])

    def swap_near(arrays):
        return [lax.ppermute(a, "width", near_pairs) for a in arrays]

    def swap_far(a):
        return lax.ppermute(a, "width", far_pairs)

    def arrange(rows):
        split = rows.reshape(2, 2, share, rows.shape[-1])
        found = []
        for lo, hi in pieces:
            cut = split[:, :, lo:hi]
            own = lax.dynamic_index_in_dim(cut, near, 1, keepdims=False)
            other = lax.dynamic_index_in_dim(cut, 1 - near, 1, keepdims=False)
            found.append(jnp.stack([own, other]).reshape(-1, model))
        return found

    x_rows = arrange(inputs[0])
    chain = Chain()
    store = [{} for _ in pieces]
    weights = {}
    saved = {}

    def size(i):
        return pieces[i][1] - pieces[i][0]

    def cut_rows(i):
        return 2 * size(i) // cuts

    def cut_shapes(i):
        return [(shape((cut_rows(i), feats)), vector)] * cuts

    def write_cuts(i, value, own, others, columns):
        n = size(i)
        own[:, columns] = value[: 2 * n]
        for k, out in enumerate(others):
            start = 2 * n + k * cut_rows(i)
            out[:, columns] = value[start : start + cut_rows(i)]

    def enter(i):
        n = size(i)

        def body(ins, outs, buffers, sems):
            x, w = ins
            own, *others, high, low = outs
            x_high, x_low = halves(x[...])

            def read(k):
                return pltpu.make_async_copy(
                    w.at[0, :, pl.ds(k * tile, tile)], buffers.at[k % 2], sems.at[k % 2]
                )

            def step(k, slot):
                columns = slice(k * tile, (k + 1) * tile)
                w_high, w_low = halves(buffers[slot])
                high[:, columns], low[:, columns] = w_high, w_low
                write_cuts(i, three(x_high, x_low, w_high, w_low, plain), own, others, columns)

            stream(tiles, read, step)

        own, *others, high, low = chain(
            "enter",
            body,
            [(x_rows[i], vector), (w_enc, hbm)],
            [(shape((2 * n, feats)), vector)]
            + cut_shapes(i)
            + [(shape((model, feats), bf16), vector)] * 2,
            scratch=[pltpu.VMEM((2, model, tile), f32), pltpu.SemaphoreType.DMA((2,))],
            limit=46,
        )
        weights["enc"] = [high, low]
        store[i]["own"], store[i]["in"] = own, swap_near(others)

    def part(i):
        n = size(i)

        def body(ins, outs):
            x, high, low = ins
            own, *others = outs
            x_high, x_low = halves(x[...])

            def step(columns):
                value = three(x_high, x_low, high[:, columns], low[:, columns], plain)
                write_cuts(i, value, own, others, columns)

            loop(feats, wide, step)

        own, *others = chain(
            "part",
            body,
            [(x_rows[i], vector)] + [(w, vector) for w in weights["enc"]],
            [(shape((2 * n, feats)), vector)] + cut_shapes(i),
        )
        store[i]["own"], store[i]["in"] = own, swap_near(others)

    def summed(i):
        n = size(i)

        def body(ins, outs):
            own, *others = ins

            def step(columns):
                outs[0][:, columns] = own[:, columns] + join(others, columns)

            loop(feats, wide, step)

        (value,) = chain(
            "chip_sum",
            body,
            [(a, vector) for a in [store[i]["own"], *store[i]["in"]]],
            [(shape((2 * n, feats)), vector)],
        )
        store[i]["sum"], store[i]["in"] = value, swap_far(value)

    def split_decoder(_):
        def body(ins, outs, buffers, sems):
            w = ins[0]
            high, low = outs

            def read(k):
                return pltpu.make_async_copy(
                    w.at[0, :, pl.ds(k * tile, tile)], buffers.at[k % 2], sems.at[k % 2]
                )

            def step(k, slot):
                rows = slice(k * tile, (k + 1) * tile)
                for t in range(2):
                    high[t, rows], low[t, rows] = halves(buffers[slot, t])

            stream(tiles, read, step)

        weights["dec"] = chain(
            "split_decoder",
            body,
            [(w_dec, hbm)],
            [(shape((2, feats, model), bf16), vector)] * 2,
            scratch=[pltpu.VMEM((2, 2, tile, model), f32), pltpu.SemaphoreType.DMA((2,))],
            limit=28,
        )

    def goals(_):
        share_rows = targets.shape[1]

        def body(ins, outs):
            flag, goal = ins
            home, away = outs
            own = flag[0] == 1
            home[...] = jnp.where(own, goal[0], goal[1])
            away[...] = jnp.where(own, goal[1], goal[0])

        home, away = chain(
            "targets",
            body,
            [(flags, scalars), (targets, vector)],
            [(shape((share_rows, model)), vector)] * 2,
        )
        away = lax.ppermute(away, "layer", [(0, 1), (1, 0)])
        padded = jnp.zeros((tokens, model), f32)
        home_start = (layer_pos * feat_size + feat_pos) * share_rows
        away_start = ((1 - layer_pos) * feat_size + feat_pos) * share_rows
        padded = lax.dynamic_update_slice(padded, home, (home_start, jnp.int32(0)))
        padded = lax.dynamic_update_slice(padded, away, (away_start, jnp.int32(0)))
        weights["goal"] = arrange(padded)

    def gate(i):
        n = size(i)

        def body(ins, outs):
            flag, s, r, b, th = ins
            *acts, slope = outs

            def step(columns):
                bias, edge = b[:, columns], th[:, columns]

                def opened(pre):
                    return jax.nn.sigmoid((pre - edge) / softness)

                for k, out in enumerate(acts):
                    rows = slice(k * cut_rows(i), (k + 1) * cut_rows(i))
                    pre = s[rows, columns] + r[rows, columns] + bias
                    out[:, columns] = pre * opened(pre)
                rows = pl.ds(pl.multiple_of(flag[1] * n, n), n)
                pre = s[rows, columns] + r[rows, columns] + bias
                own = opened(pre)
                slope[:, columns] = own + pre * own * (1.0 - own) / softness

            loop(feats, wide, step)

        *acts, slope = chain(
            "gate",
            body,
            [
                (flags, scalars),
                (store[i]["sum"], vector),
                (store[i]["in"], vector),
                (b_enc, vector),
                (thresholds, vector),
            ],
            cut_shapes(i) + [(shape((n, feats)), vector)],
        )
        store[i]["acts"], store[i]["slope"], store[i]["in"] = acts, slope, swap_near(acts)

    def recon(i):
        n = size(i)
        lo = pieces[i][0]

        def body(ins, outs, made, sem):
            own, other = ins[:cuts], ins[cuts : 2 * cuts]
            high, low = ins[2 * cuts : 2 * cuts + 2]
            r0, r1, kept = outs
            rows = pl.ds(4 * lo, 4 * n)
            r0[...] = jnp.zeros_like(r0)
            r1[...] = jnp.zeros_like(r1)

            def step(columns):
                a_high, a_low = halves(join(own + other, columns))
                made[0, :, columns], made[1, :, columns] = a_high, a_low
                pltpu.make_async_copy(
                    made.at[:, :, columns], kept.at[pl.ds(0, 2), rows, columns], sem
                ).start()
                for t, out in enumerate((r0, r1)):
                    out[...] += three(a_high, a_low, high[t, columns], low[t, columns], plain)

            loop(feats, wide, step)
            pltpu.make_async_copy(made, kept.at[pl.ds(0, 2), rows], sem).wait()

        ins = [(a, vector) for a in [*store[i]["acts"], *store[i]["in"], *weights["dec"]]]
        outs = [(shape((4 * n, model)), vector)] * 2
        aliases = {}
        if "acts" in saved:
            aliases = {len(ins): len(outs)}
            ins.append((saved["acts"], hbm))
        outs.append((shape((4, tokens, feats), bf16), hbm))
        r0, r1, saved["acts"] = chain(
            "recon",
            body,
            ins,
            outs,
            scratch=[pltpu.VMEM((2, 4 * n, feats), bf16), pltpu.SemaphoreType.DMA],
            aliases=aliases,
        )
        store[i]["r"] = (r0, r1)
        store[i]["in"] = lax.ppermute(r1, "layer", [(0, 1)])

    def held(i):
        n = size(i)

        def body(ins, outs):
            flag, r0, r1, below, goal = ins
            outs[0][...] = jnp.where(flag[0] == 1, r0[...], r1[...] + below[...]) - goal[...]

        arrays = [*store[i]["r"], store[i]["in"], weights["goal"][i]]
        (value,) = chain(
            "held",
            body,
            [(flags, scalars)] + [(a, vector) for a in arrays],
            [(shape((4 * n, model)), vector)],
        )
        store[i]["held"] = value
        if feat_size <= 4:
            store[i]["in"] = lax.ppermute(value, "feat", [(k, k ^ 1) for k in range(feat_size)])
        else:
            store[i]["in"] = lax.psum(value, "feat")
            store[i]["held"] = jnp.zeros_like(value)

    def middle(i):
        n = size(i)
        if feat_size > 4:
            return

        def body(ins, outs):
            outs[0][...] = ins[0][...] + ins[1][...]

        (value,) = chain(
            "feat_sum",
            body,
            [(store[i]["held"], vector), (store[i]["in"], vector)],
            [(shape((4 * n, model)), vector)],
        )
        store[i]["held"] = value
        store[i]["in"] = lax.ppermute(value, "feat", [(k, k ^ 2) for k in range(feat_size)])

    def across(i):
        n = size(i)

        def body(ins, outs):
            flag, a, b, bias = ins
            line = jnp.where(flag[0] == 1, bias[0:1, :], bias[1:2, :])
            outs[0][...] = a[...] + b[...] + line

        (value,) = chain(
            "errors",
            body,
            [(flags, scalars)] + [(a, vector) for a in (store[i]["held"], store[i]["in"], b_dec)],
            [(shape((4 * n, model)), vector)],
        )
        store[i]["held"] = value
        store[i]["in"] = lax.ppermute(value, "layer", [(1, 0)])

    def back(i):
        n = size(i)

        def body(ins, outs):
            flag, value, above, high, low = ins
            own, *others, e = outs
            e_high, e_low = e.at[0], e.at[1]
            is_first = flag[0] == 1
            zero = jnp.where(is_first, value[...], 0.0)
            one = jnp.where(is_first, above[...], value[...])
            e_high[:, :model], e_low[:, :model] = halves(zero)
            e_high[:, model:], e_low[:, model:] = halves(one)
            def step(columns):
                total = None
                for t in range(2):
                    cut = slice(t * model, (t + 1) * model)
                    term = three(
                        e_high[:, cut], e_low[:, cut], high[t, columns], low[t, columns], across_columns
                    )
                    total = term if total is None else total + term
                write_cuts(i, total, own, others, columns)

            loop(feats, wide, step)

        arrays = [store[i]["held"], store[i]["in"], *weights["dec"]]
        ins = [(flags, scalars)] + [(a, vector) for a in arrays]
        outs = [(shape((2 * n, feats)), vector)] + cut_shapes(i)
        outs.append((shape((2, 4 * n, 2 * model), bf16), vector))
        own, *others, store[i]["errors"] = chain("back", body, ins, outs)
        store[i]["own"], store[i]["in"] = own, swap_near(others)

    def turn(i):
        n = size(i)
        half = cuts // 2

        def body(ins, outs):
            flag, own, *others = ins
            mine, theirs = outs
            for place in range(2):

                @pl.when(flag[1] == place)
                def _():
                    for out, at in ((mine, place), (theirs, 1 - place)):

                        def step(columns):
                            arrived = join(others[at * half : (at + 1) * half], columns)
                            out[:, columns] = own[at * n : (at + 1) * n, columns] + arrived

                        loop(feats, wide, step)

        mine, theirs = chain(
            "turn",
            body,
            [(flags, scalars)] + [(a, vector) for a in [store[i]["own"], *store[i]["in"]]],
            [(shape((n, feats)), vector)] * 2,
        )
        store[i]["own"], store[i]["in"] = mine, swap_far(theirs)

    def finish(i):
        lo, hi = pieces[i]
        n = size(i)

        def body(ins, outs, value, sem):
            mine, arrived, slope = ins[:3]

            def step(columns):
                value[:, columns] = (mine[:, columns] + arrived[:, columns]) * slope[:, columns]

            loop(feats, wide, step)
            copy = pltpu.make_async_copy(value, outs[0].at[0, pl.ds(lo, n)], sem)
            copy.start()
            copy.wait()

        ins = [(store[i][k], vector) for k in ("own", "in", "slope")]
        aliases = {}
        if "grad" in saved:
            aliases = {len(ins): 0}
            ins.append((saved["grad"], hbm))
        (saved["grad"],) = chain(
            "finish",
            body,
            ins,
            [(shape((1, share, feats)), hbm)],
            scratch=[pltpu.VMEM((n, feats), f32), pltpu.SemaphoreType.DMA],
            aliases=aliases,
        )

    def decoder_grad(step):
        span = pieces[-1:] if step else pieces[:-1]
        base, rows = 4 * span[0][0], 4 * (span[-1][1] - span[0][0])
        errors = [store[pieces.index(p)]["errors"] for p in span]
        ins = [(e, vector) for e in errors] + [(saved["acts"], hbm)]
        if step and "grad" in weights:
            ins.append((weights["grad"], vector))

        def body(ins, outs, e, buffers, sems, made=None):
            out, a = outs[0], ins[len(span)]
            for (lo, hi), piece in zip(span, ins):
                e[:, 4 * lo - base : 4 * hi - base] = piece[...]

            def copy(k):
                return pltpu.make_async_copy(
                    a.at[pl.ds(0, 2), pl.ds(base, rows), pl.ds(k * tile, tile)],
                    buffers.at[k % 2],
                    sems.at[k % 2],
                )

            def write(k):
                return pltpu.make_async_copy(
                    made.at[k % 2], out.at[0, :, pl.ds(k * tile, tile)], sems.at[2 + k % 2]
                )

            def turn(k, slot):
                a_high, a_low = buffers[slot, 0], buffers[slot, 1]
                value = three(a_high, a_low, e[0], e[1], across_rows)
                features = slice(k * tile, (k + 1) * tile)
                if step and k >= 2:
                    write(k - 2).wait()
                for t in range(2):
                    term = value[:, t * model : (t + 1) * model]
                    if not step:
                        out[t, features] = term
                        continue
                    if len(ins) > len(span) + 1:
                        term = term + ins[-1][t, features]
                    made[slot, t] = term
                if step:
                    write(k).start()

            stream(tiles, copy, turn)
            if step:
                for k in range(max(tiles - 2, 0), tiles):
                    write(k).wait()

        scratch = [
            pltpu.VMEM((2, rows, 2 * model), bf16),
            pltpu.VMEM((2, 2, rows, tile), bf16),
            pltpu.SemaphoreType.DMA((4,)),
        ]
        if step:
            scratch.append(pltpu.VMEM((2, 2, tile, model), f32))
        (weights["grad"],) = chain(
            "decoder_grad",
            body,
            ins,
            [(shape((1, 2, feats, model)), hbm)] if step else [(shape((2, feats, model)), vector)],
            scratch=scratch,
            limit=22,
        )

    last = len(pieces)

    stages = {
        "enter": enter,
        "part": part,
        "sum": summed,
        "split": split_decoder,
        "goals": goals,
        "gate": gate,
        "recon": recon,
        "held": held,
        "mid": middle,
        "err": across,
        "back": back,
        "turn": turn,
        "fin": finish,
        "dg": decoder_grad,
    }
    for stage, i in order if last == len(eighths) else plain_order(last):
        stages[stage](i)
    dec_grad = weights["grad"]
    return dec_grad, saved["grad"]


def solution(mesh):
    in_specs = (
        P("layer", None, "width"),
        P(None, ("layer", "feat"), "width"),
        P("layer", "width", "feat"),
        P("layer", "feat"),
        P("layer", "feat"),
        P("layer", None, "feat", "width"),
        P(None, "width"),
    )
    out_specs = (P("layer", None, "feat", "width"), P("layer", "width", "feat"))
    return jax.shard_map(local, mesh=mesh, in_specs=in_specs, out_specs=out_specs, check_vma=False)
```

```python
import functools

import jax
import jax.numpy as jnp
from jax import lax
from jax.experimental import pallas as pl
from jax.experimental.pallas import tpu as pltpu
from jax.sharding import PartitionSpec as P

softness = 0.5
eighths = (1, 2, 2, 2, 1)
late = 2
cuts = 4
order = (
    ("enter", 0), ("sum", 0), ("part", 3), ("goals", 0), ("sum", 3), ("split", 0), ("part", 1),
    ("part", 2), ("gate", 0), ("recon", 0), ("part", 4), ("sum", 1), ("held", 0), ("mid", 0),
    ("sum", 2), ("gate", 3), ("err", 0), ("recon", 3), ("back", 0), ("held", 3), ("gate", 1),
    ("mid", 3), ("recon", 1), ("sum", 4), ("err", 3), ("turn", 0), ("held", 1), ("gate", 2),
    ("back", 3), ("mid", 1), ("recon", 2), ("turn", 3), ("held", 2), ("gate", 4), ("recon", 4),
    ("err", 1), ("held", 4), ("mid", 2), ("mid", 4), ("back", 1), ("err", 2), ("turn", 1),
    ("fin", 3), ("fin", 0), ("err", 4), ("back", 2), ("back", 4), ("turn", 2), ("fin", 1),
    ("dg", 0), ("turn", 4), ("dg", 1), ("fin", 4), ("fin", 2),
)
f32 = jnp.float32
bf16 = jnp.bfloat16
anywhere = pl.BlockSpec(memory_space=pl.ANY)
scalars = pl.BlockSpec(memory_space=pltpu.SMEM)
vector = pl.BlockSpec(memory_space=pltpu.VMEM)
hbm = pl.BlockSpec(memory_space=pltpu.HBM)
mega = 1024 * 1024


def pieces_of(rows):
    if rows % 128:
        return [(0, rows)]
    bounds = [0]
    for part in eighths:
        bounds.append(bounds[-1] + part * rows // 8)
    return list(zip(bounds[:-1], bounds[1:]))


def plain_order(count):
    found = [("enter", 0), ("split", 0), ("goals", 0)]
    for i in range(count):
        for stage in ("part", "sum", "gate", "recon", "held", "mid", "err", "back", "turn", "fin"):
            if i or stage != "part":
                found.append((stage, i))
    return found + [("dg", step) for step in range(2) if step or count > late]


def halves(value):
    high = value.astype(bf16)
    return high, (value - high.astype(f32)).astype(bf16)


def three(a_high, a_low, b_high, b_low, dims):
    dot = functools.partial(
        lax.dot_general, dimension_numbers=(dims, ((), ())), preferred_element_type=f32
    )
    return dot(a_high, b_high) + (dot(a_low, b_high) + dot(a_high, b_low))


plain = ((1,), (0,))
across_rows = ((0,), (0,))
across_columns = ((1,), (1,))


def shape(dims, kind=f32):
    return jax.ShapeDtypeStruct(dims, kind)


def loop(total, step, body):
    def turn(k, carry):
        body(pl.ds(pl.multiple_of(k * step, step), step))
        return carry

    lax.fori_loop(0, total // step, turn, 0)


def join(refs, columns):
    return jnp.concatenate([r[:, columns] for r in refs])


class Chain:
    def __init__(self):
        self.last = None

    def __call__(
        self, name, body, inputs, outputs, scratch=(), aliases=None, limit=16, grid=None
    ):
        arrays = [a for a, _ in inputs]
        in_specs = [s for _, s in inputs]
        extra = 0
        if self.last is not None:
            arrays.append(self.last)
            in_specs.append(anywhere)
            extra = 1
        count = len(inputs)
        given = len(outputs)

        def kernel(*refs):
            ins = refs[:count]
            outs = refs[count + extra : count + extra + given]
            mark = refs[count + extra + given]
            mark[...] = jnp.zeros_like(mark)
            body(ins, outs, *refs[count + extra + given + 1 :])

        mark_spec = vector if grid is None else pl.BlockSpec((8, 128), lambda *i: (0, 0))
        result = pl.pallas_call(
            kernel,
            grid=grid or (),
            in_specs=in_specs,
            out_specs=[s for _, s in outputs] + [mark_spec],
            out_shape=[o for o, _ in outputs] + [shape((8, 128))],
            scratch_shapes=list(scratch),
            input_output_aliases=aliases or {},
            compiler_params=pltpu.CompilerParams(vmem_limit_bytes=limit * mega),
            cost_estimate=pl.CostEstimate(flops=0, bytes_accessed=0, transcendentals=0),
            name=name,
        )(*arrays)
        self.last = result[-1]
        return result[:-1]


def stream(count, copy, body):
    copy(0).start()
    for k in range(count):
        if k + 1 < count:
            copy(k + 1).start()
        copy(k).wait()
        body(k, k % 2)


def local(inputs, targets, w_enc, b_enc, thresholds, w_dec, b_dec):
    layer_pos = lax.axis_index("layer")
    first = layer_pos == 0
    feat_pos = lax.axis_index("feat")
    feat_size = lax.axis_size("feat")
    width = lax.axis_size("width")
    pos = lax.axis_index("width")
    near = pos % 2
    far = pos // 2
    tokens = inputs.shape[1]
    model = inputs.shape[2]
    feats = w_enc.shape[2]
    share = tokens // width
    tile = min(512, feats)
    tiles = feats // tile
    wide = min(1024, feats)
    near_pairs = [(i, i ^ 1) for i in range(width)]
    far_pairs = [(i, i ^ 2) for i in range(width)]
    pieces = pieces_of(share)
    flags = jnp.stack([first.astype(jnp.int32), far.astype(jnp.int32)])

    def swap_near(arrays):
        return [lax.ppermute(a, "width", near_pairs) for a in arrays]

    def swap_far(a):
        return lax.ppermute(a, "width", far_pairs)

    def arrange(rows):
        split = rows.reshape(2, 2, share, rows.shape[-1])
        found = []
        for lo, hi in pieces:
            cut = split[:, :, lo:hi]
            own = lax.dynamic_index_in_dim(cut, near, 1, keepdims=False)
            other = lax.dynamic_index_in_dim(cut, 1 - near, 1, keepdims=False)
            found.append(jnp.stack([own, other]).reshape(-1, model))
        return found

    x_rows = arrange(inputs[0])
    chain = Chain()
    store = [{} for _ in pieces]
    weights = {}
    saved = {}

    def size(i):
        return pieces[i][1] - pieces[i][0]

    def cut_rows(i):
        return 2 * size(i) // cuts

    def cut_shapes(i):
        return [(shape((cut_rows(i), feats)), vector)] * cuts

    def write_cuts(i, value, own, others, columns):
        n = size(i)
        own[:, columns] = value[: 2 * n]
        for k, out in enumerate(others):
            start = 2 * n + k * cut_rows(i)
            out[:, columns] = value[start : start + cut_rows(i)]

    def enter(i):
        n = size(i)

        def body(ins, outs, buffers, sems):
            x, w = ins
            own, *others, high, low = outs
            x_high, x_low = halves(x[...])

            def read(k):
                return pltpu.make_async_copy(
                    w.at[0, :, pl.ds(k * tile, tile)], buffers.at[k % 2], sems.at[k % 2]
                )

            def step(k, slot):
                columns = slice(k * tile, (k + 1) * tile)
                w_high, w_low = halves(buffers[slot])
                high[:, columns], low[:, columns] = w_high, w_low
                write_cuts(i, three(x_high, x_low, w_high, w_low, plain), own, others, columns)

            stream(tiles, read, step)

        own, *others, high, low = chain(
            "enter",
            body,
            [(x_rows[i], vector), (w_enc, hbm)],
            [(shape((2 * n, feats)), vector)]
            + cut_shapes(i)
            + [(shape((model, feats), bf16), vector)] * 2,
            scratch=[pltpu.VMEM((2, model, tile), f32), pltpu.SemaphoreType.DMA((2,))],
            limit=46,
        )
        weights["enc"] = [high, low]
        store[i]["own"], store[i]["in"] = own, swap_near(others)

    def part(i):
        n = size(i)

        def body(ins, outs):
            x, high, low = ins
            own, *others = outs
            x_high, x_low = halves(x[...])

            def step(columns):
                value = three(x_high, x_low, high[:, columns], low[:, columns], plain)
                write_cuts(i, value, own, others, columns)

            loop(feats, wide, step)

        own, *others = chain(
            "part",
            body,
            [(x_rows[i], vector)] + [(w, vector) for w in weights["enc"]],
            [(shape((2 * n, feats)), vector)] + cut_shapes(i),
        )
        store[i]["own"], store[i]["in"] = own, swap_near(others)

    def summed(i):
        n = size(i)

        def body(ins, outs):
            own, *others = ins

            def step(columns):
                outs[0][:, columns] = own[:, columns] + join(others, columns)

            loop(feats, wide, step)

        (value,) = chain(
            "chip_sum",
            body,
            [(a, vector) for a in [store[i]["own"], *store[i]["in"]]],
            [(shape((2 * n, feats)), vector)],
        )
        store[i]["sum"], store[i]["in"] = value, swap_far(value)

    def split_decoder(_):
        def body(ins, outs, buffers, sems):
            w = ins[0]
            high, low = outs

            def read(k):
                return pltpu.make_async_copy(
                    w.at[0, :, pl.ds(k * tile, tile)], buffers.at[k % 2], sems.at[k % 2]
                )

            def step(k, slot):
                rows = slice(k * tile, (k + 1) * tile)
                for t in range(2):
                    high[t, rows], low[t, rows] = halves(buffers[slot, t])

            stream(tiles, read, step)

        weights["dec"] = chain(
            "split_decoder",
            body,
            [(w_dec, hbm)],
            [(shape((2, feats, model), bf16), vector)] * 2,
            scratch=[pltpu.VMEM((2, 2, tile, model), f32), pltpu.SemaphoreType.DMA((2,))],
            limit=28,
        )

    def goals(_):
        share_rows = targets.shape[1]

        def body(ins, outs):
            flag, goal = ins
            home, away = outs
            own = flag[0] == 1
            home[...] = jnp.where(own, goal[0], goal[1])
            away[...] = jnp.where(own, goal[1], goal[0])

        home, away = chain(
            "targets",
            body,
            [(flags, scalars), (targets, vector)],
            [(shape((share_rows, model)), vector)] * 2,
        )
        away = lax.ppermute(away, "layer", [(0, 1), (1, 0)])
        padded = jnp.zeros((tokens, model), f32)
        home_start = (layer_pos * feat_size + feat_pos) * share_rows
        away_start = ((1 - layer_pos) * feat_size + feat_pos) * share_rows
        padded = lax.dynamic_update_slice(padded, home, (home_start, jnp.int32(0)))
        padded = lax.dynamic_update_slice(padded, away, (away_start, jnp.int32(0)))
        weights["goal"] = arrange(padded)

    def gate(i):
        n = size(i)

        def body(ins, outs):
            flag, s, r, b, th = ins
            *acts, slope = outs

            def step(columns):
                bias, edge = b[:, columns], th[:, columns]

                def opened(pre):
                    return jax.nn.sigmoid((pre - edge) / softness)

                for k, out in enumerate(acts):
                    rows = slice(k * cut_rows(i), (k + 1) * cut_rows(i))
                    pre = s[rows, columns] + r[rows, columns] + bias
                    out[:, columns] = pre * opened(pre)
                rows = pl.ds(pl.multiple_of(flag[1] * n, n), n)
                pre = s[rows, columns] + r[rows, columns] + bias
                own = opened(pre)
                slope[:, columns] = own + pre * own * (1.0 - own) / softness

            loop(feats, wide, step)

        *acts, slope = chain(
            "gate",
            body,
            [
                (flags, scalars),
                (store[i]["sum"], vector),
                (store[i]["in"], vector),
                (b_enc, vector),
                (thresholds, vector),
            ],
            cut_shapes(i) + [(shape((n, feats)), vector)],
        )
        store[i]["acts"], store[i]["slope"], store[i]["in"] = acts, slope, swap_near(acts)

    def recon(i):
        n = size(i)
        lo = pieces[i][0]

        def body(ins, outs, made, sem):
            own, other = ins[:cuts], ins[cuts : 2 * cuts]
            high, low = ins[2 * cuts : 2 * cuts + 2]
            r0, r1, kept = outs
            rows = pl.ds(4 * lo, 4 * n)
            r0[...] = jnp.zeros_like(r0)
            r1[...] = jnp.zeros_like(r1)

            def step(columns):
                a_high, a_low = halves(join(own + other, columns))
                made[0, :, columns], made[1, :, columns] = a_high, a_low
                pltpu.make_async_copy(
                    made.at[:, :, columns], kept.at[pl.ds(0, 2), rows, columns], sem
                ).start()
                for t, out in enumerate((r0, r1)):
                    out[...] += three(a_high, a_low, high[t, columns], low[t, columns], plain)

            loop(feats, wide, step)
            pltpu.make_async_copy(made, kept.at[pl.ds(0, 2), rows], sem).wait()

        ins = [(a, vector) for a in [*store[i]["acts"], *store[i]["in"], *weights["dec"]]]
        outs = [(shape((4 * n, model)), vector)] * 2
        aliases = {}
        if "acts" in saved:
            aliases = {len(ins): len(outs)}
            ins.append((saved["acts"], hbm))
        outs.append((shape((4, tokens, feats), bf16), hbm))
        r0, r1, saved["acts"] = chain(
            "recon",
            body,
            ins,
            outs,
            scratch=[pltpu.VMEM((2, 4 * n, feats), bf16), pltpu.SemaphoreType.DMA],
            aliases=aliases,
        )
        store[i]["r"] = (r0, r1)
        store[i]["in"] = lax.ppermute(r1, "layer", [(0, 1)])

    def held(i):
        n = size(i)

        def body(ins, outs):
            flag, r0, r1, below, goal = ins
            outs[0][...] = jnp.where(flag[0] == 1, r0[...], r1[...] + below[...]) - goal[...]

        arrays = [*store[i]["r"], store[i]["in"], weights["goal"][i]]
        (value,) = chain(
            "held",
            body,
            [(flags, scalars)] + [(a, vector) for a in arrays],
            [(shape((4 * n, model)), vector)],
        )
        store[i]["held"] = value
        if feat_size <= 4:
            store[i]["in"] = lax.ppermute(value, "feat", [(k, k ^ 1) for k in range(feat_size)])
        else:
            store[i]["in"] = lax.psum(value, "feat")
            store[i]["held"] = jnp.zeros_like(value)

    def middle(i):
        n = size(i)
        if feat_size > 4:
            return

        def body(ins, outs):
            outs[0][...] = ins[0][...] + ins[1][...]

        (value,) = chain(
            "feat_sum",
            body,
            [(store[i]["held"], vector), (store[i]["in"], vector)],
            [(shape((4 * n, model)), vector)],
        )
        store[i]["held"] = value
        store[i]["in"] = lax.ppermute(value, "feat", [(k, k ^ 2) for k in range(feat_size)])

    def across(i):
        n = size(i)

        def body(ins, outs):
            flag, a, b, bias = ins
            line = jnp.where(flag[0] == 1, bias[0:1, :], bias[1:2, :])
            outs[0][...] = a[...] + b[...] + line

        (value,) = chain(
            "errors",
            body,
            [(flags, scalars)] + [(a, vector) for a in (store[i]["held"], store[i]["in"], b_dec)],
            [(shape((4 * n, model)), vector)],
        )
        store[i]["held"] = value
        store[i]["in"] = lax.ppermute(value, "layer", [(1, 0)])

    def back(i):
        n = size(i)

        def body(ins, outs):
            flag, value, above, high, low = ins
            own, *others, e = outs
            e_high, e_low = e.at[0], e.at[1]
            is_first = flag[0] == 1
            zero = jnp.where(is_first, value[...], 0.0)
            one = jnp.where(is_first, above[...], value[...])
            e_high[:, :model], e_low[:, :model] = halves(zero)
            e_high[:, model:], e_low[:, model:] = halves(one)
            def step(columns):
                total = None
                for t in range(2):
                    cut = slice(t * model, (t + 1) * model)
                    term = three(
                        e_high[:, cut], e_low[:, cut], high[t, columns], low[t, columns], across_columns
                    )
                    total = term if total is None else total + term
                write_cuts(i, total, own, others, columns)

            loop(feats, wide, step)

        arrays = [store[i]["held"], store[i]["in"], *weights["dec"]]
        ins = [(flags, scalars)] + [(a, vector) for a in arrays]
        outs = [(shape((2 * n, feats)), vector)] + cut_shapes(i)
        outs.append((shape((2, 4 * n, 2 * model), bf16), vector))
        own, *others, store[i]["errors"] = chain("back", body, ins, outs)
        store[i]["own"], store[i]["in"] = own, swap_near(others)

    def turn(i):
        n = size(i)
        half = cuts // 2

        def body(ins, outs):
            flag, own, *others = ins
            mine, theirs = outs
            for place in range(2):

                @pl.when(flag[1] == place)
                def _():
                    for out, at in ((mine, place), (theirs, 1 - place)):

                        def step(columns):
                            arrived = join(others[at * half : (at + 1) * half], columns)
                            out[:, columns] = own[at * n : (at + 1) * n, columns] + arrived

                        loop(feats, wide, step)

        mine, theirs = chain(
            "turn",
            body,
            [(flags, scalars)] + [(a, vector) for a in [store[i]["own"], *store[i]["in"]]],
            [(shape((n, feats)), vector)] * 2,
        )
        store[i]["own"], store[i]["in"] = mine, swap_far(theirs)

    def finish(i):
        lo, hi = pieces[i]
        n = size(i)

        def body(ins, outs, value, sem):
            mine, arrived, slope = ins[:3]

            def step(columns):
                value[:, columns] = (mine[:, columns] + arrived[:, columns]) * slope[:, columns]

            loop(feats, wide, step)
            copy = pltpu.make_async_copy(value, outs[0].at[0, pl.ds(lo, n)], sem)
            copy.start()
            copy.wait()

        ins = [(store[i][k], vector) for k in ("own", "in", "slope")]
        aliases = {}
        if "grad" in saved:
            aliases = {len(ins): 0}
            ins.append((saved["grad"], hbm))
        (saved["grad"],) = chain(
            "finish",
            body,
            ins,
            [(shape((1, share, feats)), hbm)],
            scratch=[pltpu.VMEM((n, feats), f32), pltpu.SemaphoreType.DMA],
            aliases=aliases,
        )

    def decoder_grad(step):
        span = pieces[-late:] if step else pieces[:-late]
        base, rows = 4 * span[0][0], 4 * (span[-1][1] - span[0][0])
        errors = [store[pieces.index(p)]["errors"] for p in span]
        ins = [(e, vector) for e in errors] + [(saved["acts"], hbm)]
        if step and "grad" in weights:
            ins.append((weights["grad"], vector))

        def body(ins, outs, e, buffers, sems, made=None):
            out, a = outs[0], ins[len(span)]
            for (lo, hi), piece in zip(span, ins):
                e[:, 4 * lo - base : 4 * hi - base] = piece[...]

            def copy(k):
                return pltpu.make_async_copy(
                    a.at[pl.ds(0, 2), pl.ds(base, rows), pl.ds(k * tile, tile)],
                    buffers.at[k % 2],
                    sems.at[k % 2],
                )

            def write(k):
                return pltpu.make_async_copy(
                    made.at[k % 2], out.at[0, :, pl.ds(k * tile, tile)], sems.at[2 + k % 2]
                )

            def turn(k, slot):
                a_high, a_low = buffers[slot, 0], buffers[slot, 1]
                value = three(a_high, a_low, e[0], e[1], across_rows)
                features = slice(k * tile, (k + 1) * tile)
                if step and k >= 2:
                    write(k - 2).wait()
                for t in range(2):
                    term = value[:, t * model : (t + 1) * model]
                    if not step:
                        out[t, features] = term
                        continue
                    if len(ins) > len(span) + 1:
                        term = term + ins[-1][t, features]
                    made[slot, t] = term
                if step:
                    write(k).start()

            stream(tiles, copy, turn)
            if step:
                for k in range(max(tiles - 2, 0), tiles):
                    write(k).wait()

        scratch = [
            pltpu.VMEM((2, rows, 2 * model), bf16),
            pltpu.VMEM((2, 2, rows, tile), bf16),
            pltpu.SemaphoreType.DMA((4,)),
        ]
        if step:
            scratch.append(pltpu.VMEM((2, 2, tile, model), f32))
        (weights["grad"],) = chain(
            "decoder_grad",
            body,
            ins,
            [(shape((1, 2, feats, model)), hbm)] if step else [(shape((2, feats, model)), vector)],
            scratch=scratch,
            limit=22,
        )

    last = len(pieces)

    stages = {
        "enter": enter,
        "part": part,
        "sum": summed,
        "split": split_decoder,
        "goals": goals,
        "gate": gate,
        "recon": recon,
        "held": held,
        "mid": middle,
        "err": across,
        "back": back,
        "turn": turn,
        "fin": finish,
        "dg": decoder_grad,
    }
    for stage, i in order if last == len(eighths) else plain_order(last):
        stages[stage](i)
    dec_grad = weights["grad"]
    return dec_grad, saved["grad"]


def solution(mesh):
    in_specs = (
        P("layer", None, "width"),
        P(None, ("layer", "feat"), "width"),
        P("layer", "width", "feat"),
        P("layer", "feat"),
        P("layer", "feat"),
        P("layer", None, "feat", "width"),
        P(None, "width"),
    )
    out_specs = (P("layer", None, "feat", "width"), P("layer", "width", "feat"))
    return jax.shard_map(local, mesh=mesh, in_specs=in_specs, out_specs=out_specs, check_vma=False)
```
